32 devices in a mesh: section: 4 (over z), tp: 8 (over y, x, core).
Axes of the slice: x: 2, y: 2, z: 4, core: 2. Of those that a mesh axis runs over, the one named last changes fastest.
Arguments:
- stash: bfloat16 [4, 4, 192, 1024], P('section', None, 'tp'), may hold values from -6 to 6
- w_in: bfloat16 [4, 1024, 65536], P('section', None, 'tp'), may hold values from -0.1875 to 0.1875
- w_out: bfloat16 [4, 65536, 1024], P('section', 'tp'), may hold values from -0.0234375 to 0.0234375
- gain: float32 [4, 1024], P('section'), may hold values from 0.1 to 1.9
- plan: int32 [3, 4], replicated, may hold values from 0 to 3
- arriving: bfloat16 [4, 192, 1024], P('section', 'tp'), may hold values from -6 to 6
- fresh: bfloat16 [2, 192, 1024], P(None, 'tp'), may hold values from -6 to 6
Outputs:
- input_grads: bfloat16 [3, 4, 192, 1024], P(None, 'section', 'tp')
The draws below stay inside these ranges and needn't reach their ends.
All inputs are finite; a program needn't handle non-finite values.
Results may differ from the reference program's by a relative error of at most 0.0085.
Values may be sent and summed in bfloat16 or wider, within the bound.
No kernel may reach another device: no remote copies, remote signals or barrier semaphores. Data moves between devices by JAX's collectives and lax.ppermute only.
A program may use at most 128 MiB of HBM per device.

```python
import jax
import jax.numpy as jnp
from jax import lax

D = 1024
FF = 65536
TOK = 192
SLOTS = 4
TICKS = 3
SECTIONS = 4


def touch_ends(values, stream_key, low, largest):
    longest = values.shape.index(max(values.shape))
    spots = []
    for shift in (0, 1):
        where = [jax.random.randint(jax.random.fold_in(stream_key, axis), (), 0, length) for axis, length in enumerate(values.shape)]
        where[longest] = (where[longest] + shift) % values.shape[longest]
        spots.append(tuple(where))
    return values.at[spots[0]].set(low).at[spots[1]].set(largest)


def level_of(stream_key, shape, cuts, low, top_value):
    factor_of = 1.0
    for dim, parts in cuts:
        steps = jax.random.uniform(jax.random.fold_in(jax.random.fold_in(stream_key, 6), dim), (parts,), jnp.float32, low / len(cuts), top_value / len(cuts))
        factor_of = factor_of * jnp.repeat(jnp.exp(steps), shape[dim] // parts).reshape((-1,) + (1,) * (len(shape) - 1 - dim))
    return factor_of


def gaussian(rng, extent, deviation, most, shards=(), dtype=jnp.bfloat16):
    array = jax.random.normal(rng, extent, jnp.float32) * deviation
    if len(shards) > 0:
        array = level_of(rng, extent, shards, -0.22, 0.18) * array
    return jnp.clip(array, min=-most, max=most).astype(dtype)


def setup_inputs(seed: int = 0) -> dict:
    key_of = jax.random.split(jax.random.key(seed), 8)
    return {
        "stash": gaussian(key_of[0], (SECTIONS, SLOTS, TOK, D), 1.0, 6.0, ((0, 4), (2, 8))),
        "w_in": gaussian(key_of[1], (SECTIONS, D, FF), D ** -0.5, 0.1875, ((0, 4), (2, 8))),
        "w_out": gaussian(key_of[2], (SECTIONS, FF, D), FF ** -0.5, 0.0234375, ((0, 4), (1, 8))),
        "gain": jnp.clip(1.0 + 0.18 * jax.random.normal(key_of[3], (SECTIONS, D), jnp.float32), 0.1, 1.9),
        "plan": touch_ends(jax.random.randint(key_of[4], (TICKS, SECTIONS), 0, SLOTS), jax.random.fold_in(key_of[4], 1), 0, SLOTS - 1).astype(jnp.int32),
        "arriving": gaussian(key_of[5], (SECTIONS, TOK, D), 1.0, 6.0, ((0, 4), (1, 8))),
        "fresh": gaussian(key_of[6], (TICKS - 1, TOK, D), 1.0, 6.0, ((1, 8),)),
    }


epsilon = 1e-06

def norm_parts(x_rows):
    values = x_rows.astype(jnp.float32)
    inverse_rms = lax.rsqrt(lax.optimization_barrier(jnp.mean(values * values, axis=-1, keepdims=True)) + epsilon)
    return (inverse_rms, values * inverse_rms)

def norm_back(normed_grad, incoming, inverse_rms, normed, gain_row):
    scaled = normed_grad * gain_row
    inner = lax.optimization_barrier(jnp.mean(scaled * normed, axis=-1, keepdims=True))
    return (incoming.astype(jnp.float32) + inverse_rms * (scaled - normed * inner)).astype(jnp.bfloat16)

def section_grad(x_rows, incoming, weight_in, weight_out, gain_row):
    inverse_rms, normed = norm_parts(x_rows)
    inputs = (normed * gain_row).astype(jnp.bfloat16)
    preact = jnp.dot(inputs, weight_in, preferred_element_type=jnp.float32)
    hidden_back = jnp.dot(incoming, weight_out.T, preferred_element_type=jnp.float32)
    hidden_grad = (hidden_back * (2.0 * jnp.maximum(preact, 0.0))).astype(jnp.bfloat16)
    normed_grad = jnp.dot(hidden_grad, weight_in.T, preferred_element_type=jnp.float32)
    return norm_back(normed_grad, incoming, inverse_rms, normed, gain_row)

def reference(stash, w_in, w_out, gain, plan, arriving, fresh):
    results = []
    incoming_all = arriving
    for tick in range(TICKS):
        section_grads = []
        for section_index in range(SECTIONS):
            keeper = (section_index + SECTIONS // 2) % SECTIONS
            x_rows = stash[keeper, plan[tick, section_index]]
            section_grads.append(section_grad(x_rows, incoming_all[section_index], w_in[section_index], w_out[section_index], gain[section_index]))
        section_grads = jnp.stack(section_grads)
        results.append(section_grads)
        if tick + 1 < TICKS:
            incoming_all = jnp.concatenate([section_grads[1:], fresh[tick][None]], axis=0)
    return jnp.stack(results)
```

```python
import functools

import jax
import jax.numpy as jnp
from jax import lax
from jax.experimental import pallas as pl
from jax.experimental.pallas import tpu as pltpu
from jax.sharding import PartitionSpec as P

epsilon = 1e-06
MIB = 2**20
f32 = jnp.float32
bf16 = jnp.bfloat16
VMEM = pl.BlockSpec(memory_space=pltpu.VMEM)
HBM = pl.BlockSpec(memory_space=pltpu.HBM)
SMEM = pl.BlockSpec(memory_space=pltpu.SMEM)


def shape_of(shape, dtype):
    return jax.ShapeDtypeStruct(shape, dtype)


def limit(mib):
    return pltpu.CompilerParams(vmem_limit_bytes=mib * MIB)


def swapped(value, mask):
    return lax.ppermute(value, "tp", [(i, i ^ mask) for i in range(lax.axis_size("tp"))])


def from_mirror(value):
    count = lax.axis_size("section")
    return lax.ppermute(value, "section", [(i, (i + count // 2) % count) for i in range(count)])


def from_above(value, mask):
    sections, parts = lax.axis_size("section"), lax.axis_size("tp")
    pairs = [
        (((s + 1) % sections) * parts + (i ^ mask), s * parts + i)
        for s in range(sections)
        for i in range(parts)
    ]
    return lax.ppermute(value, ("section", "tp"), pairs)


def with_cores(chips):
    return chips + [swapped(value, 1) for value in chips]


def gathered(value):
    masks = range(2, lax.axis_size("tp"), 2)
    return with_cores([value] + [swapped(value, mask) for mask in masks])


def pick_kernel(plan, stash, first, later):
    sections = lax.axis_size("section")
    partner = lax.rem(lax.axis_index("section") + sections // 2, sections)
    first[...] = stash[0, plan[0, partner]]
    for tick in range(1, plan.shape[0]):
        later[tick - 1] = stash[0, plan[tick, partner]]


def pick(plan, stash):
    ticks, (_, _, rows, width) = plan.shape[0], stash.shape
    return pl.pallas_call(
        pick_kernel,
        out_shape=(
            shape_of((rows, width), stash.dtype),
            shape_of((ticks - 1, rows, width), stash.dtype),
        ),
        in_specs=[SMEM, VMEM],
        out_specs=(VMEM, VMEM),
        name="pick",
    )(plan, stash)


def joined(blocks):
    return jnp.concatenate([block[...].astype(f32) for block in blocks], axis=0)


def kernel_blocks(blocks):
    if blocks[0].shape[0] % 8 == 0:
        return list(blocks)
    return [jnp.concatenate(blocks, axis=0)]


def normalised(values):
    inverse_rms = lax.rsqrt(jnp.mean(values * values, axis=-1, keepdims=True) + epsilon)
    return inverse_rms, values * inverse_rms


def gate_kernel(count, *refs):
    blocks, (gain, w_in, out, inputs) = refs[:count], refs[count:]

    @pl.when(pl.program_id(0) == 0)
    def _():
        inputs[...] = (normalised(joined(blocks))[1] * gain[...]).astype(bf16)

    preact = jnp.dot(inputs[...], w_in[...], preferred_element_type=f32)
    out[...] = (2.0 * jnp.maximum(preact, 0.0)).T.astype(bf16)


def gate(blocks, gain, w_in, chunk):
    blocks = kernel_blocks(blocks)
    tokens = sum(block.shape[0] for block in blocks)
    width, hidden = w_in.shape
    chunk = min(chunk, hidden)
    return pl.pallas_call(
        functools.partial(gate_kernel, len(blocks)),
        out_shape=shape_of((hidden, tokens), bf16),
        grid=(hidden // chunk,),
        in_specs=[VMEM] * len(blocks) + [VMEM, pl.BlockSpec((width, chunk), lambda i: (0, i))],
        out_specs=pl.BlockSpec((chunk, tokens), lambda i: (i, 0)),
        scratch_shapes=[pltpu.VMEM((tokens, width), bf16)],
        compiler_params=limit(24),
        cost_estimate=pl.CostEstimate(
            flops=2 * tokens * width * hidden,
            bytes_accessed=2 * width * hidden + 2 * tokens * hidden,
            transcendentals=0,
        ),
        name="gate",
    )(*blocks, gain, w_in)


def back_kernel(count, chunk, *refs):
    blocks, (gates, w_out, w_in, own, other, gates_v, out_v, in_v, total, sems) = (
        refs[:count],
        refs[count:],
    )
    steps = gates.shape[0] // chunk
    copies = []
    for step in range(steps):
        part = pl.ds(step * chunk, chunk)
        copies.append(
            (
                pltpu.make_async_copy(w_out.at[part, :], out_v.at[part, :], sems.at[0, step]),
                pltpu.make_async_copy(gates.at[part, :], gates_v.at[part, :], sems.at[1, step]),
                pltpu.make_async_copy(w_in.at[:, part], in_v.at[:, part], sems.at[2, step]),
            )
        )
    for group in copies:
        for copy in group:
            copy.start()
    incoming = joined(blocks).T.astype(bf16)
    for step in range(steps):
        part = pl.ds(step * chunk, chunk)
        copies[step][0].wait()
        hidden_back = jnp.dot(out_v[part, :], incoming, preferred_element_type=f32)
        copies[step][1].wait()
        hidden_grad = (hidden_back * gates_v[part, :].astype(f32)).astype(bf16)
        copies[step][2].wait()
        partial = jnp.dot(in_v[:, part], hidden_grad, preferred_element_type=f32)
        if step == 0:
            total[...] = partial
        else:
            total[...] += partial
    sums = total[...].T
    half = own.shape[0]
    own[...] = sums[:half]
    other[...] = sums[half:].astype(bf16)


def back(blocks, gates, w_out, w_in, chunk):
    blocks = kernel_blocks(blocks)
    hidden, tokens = gates.shape
    width = w_in.shape[0]
    chunk = min(chunk, hidden)
    return pl.pallas_call(
        functools.partial(back_kernel, len(blocks), chunk),
        out_shape=(
            shape_of((tokens // 2, width), f32),
            shape_of((tokens // 2, width), bf16),
        ),
        in_specs=[VMEM] * len(blocks) + [HBM] * 3,
        out_specs=(VMEM, VMEM),
        scratch_shapes=[
            pltpu.VMEM((hidden, tokens), bf16),
            pltpu.VMEM((hidden, width), bf16),
            pltpu.VMEM((width, hidden), bf16),
            pltpu.VMEM((width, tokens), f32),
            pltpu.SemaphoreType.DMA((3, hidden // chunk)),
        ],
        compiler_params=limit(48),
        cost_estimate=pl.CostEstimate(
            flops=4 * tokens * width * hidden,
            bytes_accessed=4 * width * hidden + 2 * tokens * hidden,
            transcendentals=0,
        ),
        name="back",
    )(*blocks, gates, w_out, w_in)


def fold_values(own, received, rows):
    sums = own + received.astype(f32)
    return [sums[:rows]] + [
        sums[at : at + rows].astype(bf16) for at in range(rows, sums.shape[0], rows)
    ]


def fold_kernel(rows, own, received, *outs):
    for out, value in zip(outs, fold_values(own[...], received[...], rows)):
        out[...] = value


def fold(own, received, rows):
    if rows % 8:
        return fold_values(own, received, rows)
    half, width = own.shape
    return pl.pallas_call(
        functools.partial(fold_kernel, rows),
        out_shape=tuple(
            shape_of((rows, width), bf16 if at else f32) for at in range(half // rows)
        ),
        in_specs=[VMEM] * 2,
        out_specs=tuple([VMEM] * (half // rows)),
        name="fold",
    )(own, received)


def finish_kernel(ending, *refs):
    own, incoming, x_rows, gain, extra = refs[:5]
    received, outs = (refs[5:-1], refs[-1:]) if ending else (refs[5:-2], refs[-2:])
    if ending:
        past, received = received[:ending], received[ending:]
    total = own[...]
    for block in received:
        total = total + block[...].astype(f32)
    inverse_rms, normed = normalised(x_rows[...].astype(f32))
    scaled = total * gain[...]
    inner = jnp.mean(scaled * normed, axis=-1, keepdims=True)
    result = (incoming[...].astype(f32) + inverse_rms * (scaled - normed * inner)).astype(bf16)
    if ending:
        for tick in range(ending):
            outs[0][tick, 0] = past[tick][...]
        outs[0][ending, 0] = result
    else:
        outs[0][...] = result
        outs[1][...] = jnp.where(lax.axis_index("section") == 0, extra[...], result)


def finish(own, received, incoming, x_rows, gain, fresh, past=None):
    rows, width = own.shape
    ending = 0 if past is None else len(past)
    block = shape_of((rows, width), bf16)
    whole = shape_of((ending + 1, 1, rows, width), bf16)
    operands = [own, incoming, x_rows, gain, gain if ending else fresh]
    operands += (past if ending else []) + list(received)
    return pl.pallas_call(
        functools.partial(finish_kernel, ending),
        out_shape=whole if ending else (block, block),
        in_specs=[VMEM] * len(operands),
        out_specs=VMEM if ending else (VMEM, VMEM),
        name="finish",
    )(*operands)


def body(stash, w_in, w_out, gain, plan, arriving, fresh):
    ticks, rows = plan.shape[0], stash.shape[2]
    weight_in, weight_out = w_in[0], w_out[0]
    masks = range(2, lax.axis_size("tp"), 2)
    first, later = pick(plan, stash)
    incoming = gathered(arriving[0])
    x_now = gathered(from_mirror(first))
    x_later = gathered(from_mirror(later))
    gates = gate(x_now, gain, weight_in, 2048)
    results = []
    for tick in range(ticks):
        own, other = back(incoming, gates, weight_out, weight_in, 1024)
        blocks = fold(own, swapped(other, 1), rows)
        received = [swapped(block, mask) for block, mask in zip(blocks[1:], masks)]
        if tick + 1 == ticks:
            return finish(blocks[0], received, incoming[0], x_now[0], gain, None, results)
        result, outgoing = finish(
            blocks[0], received, incoming[0], x_now[0], gain, fresh[tick]
        )
        results.append(result)
        x_now = [block[tick] for block in x_later]
        gates = gate(x_now, gain, weight_in, 2048)
        incoming = with_cores([from_above(outgoing, mask) for mask in [0, *masks]])


def solution(mesh):
    placed = (
        P("section", None, "tp", None),
        P("section", None, "tp"),
        P("section", "tp", None),
        P("section", None),
        P(),
        P("section", "tp", None),
        P(None, "tp", None),
    )
    return jax.shard_map(
        body, mesh=mesh, in_specs=placed, out_specs=P(None, "section", "tp", None), check_vma=False
    )
```

```python
import functools

import jax
import jax.numpy as jnp
from jax import lax
from jax.experimental import pallas as pl
from jax.experimental.pallas import tpu as pltpu
from jax.sharding import PartitionSpec as P

epsilon = 1e-06
MIB = 2**20
f32 = jnp.float32
bf16 = jnp.bfloat16
VMEM = pl.BlockSpec(memory_space=pltpu.VMEM)
HBM = pl.BlockSpec(memory_space=pltpu.HBM)
SMEM = pl.BlockSpec(memory_space=pltpu.SMEM)
ANY = pl.BlockSpec(memory_space=pl.ANY)


def shape_of(shape, dtype):
    return jax.ShapeDtypeStruct(shape, dtype)


def limit(mib):
    return pltpu.CompilerParams(vmem_limit_bytes=mib * MIB)


def in_vmem(value):
    return pltpu.with_memory_space_constraint(value, pltpu.VMEM)


def swapped(value, mask):
    return lax.ppermute(value, "tp", [(i, i ^ mask) for i in range(lax.axis_size("tp"))])


def from_mirror(value):
    count = lax.axis_size("section")
    return lax.ppermute(value, "section", [(i, (i + count // 2) % count) for i in range(count)])


def from_above(value, mask):
    sections, parts = lax.axis_size("section"), lax.axis_size("tp")
    pairs = [
        (((s + 1) % sections) * parts + (i ^ mask), s * parts + i)
        for s in range(sections)
        for i in range(parts)
    ]
    return lax.ppermute(value, ("section", "tp"), pairs)


def with_cores(chips):
    return chips + [swapped(value, 1) for value in chips]


def gathered(value):
    masks = range(2, lax.axis_size("tp"), 2)
    return with_cores([value] + [swapped(value, mask) for mask in masks])


def pick_kernel(plan, stash, first, later):
    sections = lax.axis_size("section")
    partner = lax.rem(lax.axis_index("section") + sections // 2, sections)
    first[...] = stash[0, plan[0, partner]]
    for tick in range(1, plan.shape[0]):
        later[tick - 1] = stash[0, plan[tick, partner]]


def pick(plan, stash):
    ticks, (_, _, rows, width) = plan.shape[0], stash.shape
    return pl.pallas_call(
        pick_kernel,
        out_shape=(
            shape_of((rows, width), stash.dtype),
            shape_of((ticks - 1, rows, width), stash.dtype),
        ),
        in_specs=[SMEM, VMEM],
        out_specs=(VMEM, VMEM),
        compiler_params=limit(2),
        name="pick",
    )(plan, stash)


def load_kernel(starts, weight, after, out, token, sem):
    rows, columns = out.shape
    part = weight.at[0, pl.ds(starts[0], rows), pl.ds(starts[1], columns)]
    copy = pltpu.make_async_copy(part, out, sem)
    copy.start()
    token[...] = jnp.zeros_like(token)
    copy.wait()


def load(weight, starts, shape, after):
    return pl.pallas_call(
        functools.partial(load_kernel, starts),
        out_shape=(pltpu.VMEM(shape, weight.dtype), shape_of((8, 128), f32)),
        in_specs=[HBM, ANY],
        out_specs=(VMEM, VMEM),
        scratch_shapes=[pltpu.SemaphoreType.DMA],
        compiler_params=limit(2),
        cost_estimate=pl.CostEstimate(
            flops=0, bytes_accessed=4 * shape[0] * shape[1], transcendentals=0
        ),
        name="load",
    )(pltpu.with_memory_space_constraint(weight, pltpu.HBM), after)


def pack_kernel(first, second, after, out):
    out[0] = first[...]
    out[1] = second[0]


def pack(first, second, after):
    return pl.pallas_call(
        pack_kernel,
        out_shape=shape_of((2, *first.shape), first.dtype),
        in_specs=[VMEM, VMEM, ANY],
        out_specs=VMEM,
        compiler_params=limit(2),
        name="pack",
    )(first, second, after)


def joined(blocks, at):
    return jnp.concatenate([block[at].astype(f32) for block in blocks], axis=0)


def kernel_blocks(blocks):
    if blocks[0].shape[1] % 8 == 0:
        return list(blocks)
    return [jnp.concatenate(blocks, axis=1)]


def normalised(values):
    inverse_rms = lax.rsqrt(jnp.mean(values * values, axis=-1, keepdims=True) + epsilon)
    return inverse_rms, values * inverse_rms


def gate_values(inputs, w_in, part):
    preact = jnp.dot(inputs, w_in[:, part], preferred_element_type=f32)
    return (2.0 * jnp.maximum(preact, 0.0)).T


def spans(size, chunk):
    return [pl.ds(at, min(chunk, size)) for at in range(0, size, min(chunk, size))]


def gate_kernel(count, at, chunk, *refs):
    blocks, (gain, w_in, after, out) = refs[:count], refs[count:]
    inputs = (normalised(joined(blocks, at))[1] * gain[...]).astype(bf16)
    for part in spans(out.shape[0], chunk):
        out[part, :] = gate_values(inputs, w_in, part).astype(bf16)


def gate(blocks, at, gain, w_in, chunk, after):
    blocks = kernel_blocks(blocks)
    tokens = sum(block.shape[1] for block in blocks)
    width, hidden = w_in.shape
    return pl.pallas_call(
        functools.partial(gate_kernel, len(blocks), at, chunk),
        out_shape=pltpu.VMEM((hidden, tokens), bf16),
        in_specs=[VMEM] * (len(blocks) + 2) + [ANY],
        out_specs=VMEM,
        compiler_params=limit(6),
        cost_estimate=pl.CostEstimate(
            flops=2 * tokens * width * hidden,
            bytes_accessed=2 * width * hidden + 2 * tokens * hidden,
            transcendentals=0,
        ),
        name="gate",
    )(*blocks, gain, in_vmem(w_in), after)


def back_kernel(count, halves, chunk, at, *refs):
    blocks, refs = refs[:count], refs[count:]
    w_outs, w_ins, refs = refs[:halves], refs[halves : 2 * halves], refs[2 * halves :]
    if at is None:
        gates, (own, other) = refs[:halves], refs[halves:]
        incoming = joined(blocks, ...).T.astype(bf16)
    else:
        gain, own, other = refs
        inputs = (normalised(joined(blocks, 0))[1] * gain[...]).astype(bf16)
        incoming = joined(blocks, 1).T.astype(bf16)
    total = None
    for half in range(halves):
        for part in spans(w_outs[half].shape[0], chunk):
            hidden_back = jnp.dot(w_outs[half][part, :], incoming, preferred_element_type=f32)
            if at is None:
                factor = gates[half][part, :].astype(f32)
            else:
                factor = gate_values(inputs, w_ins[half], part)
            hidden_grad = (hidden_back * factor).astype(bf16)
            partial = jnp.dot(w_ins[half][:, part], hidden_grad, preferred_element_type=f32)
            total = partial if total is None else total + partial
    sums = total.T
    rows = own.shape[0]
    own[...] = sums[:rows]
    other[...] = sums[rows:].astype(bf16)


def back(blocks, gates, gain, w_outs, w_ins, chunk):
    paired = gates is None
    if paired:
        blocks = kernel_blocks(blocks)
    elif blocks[0].shape[0] % 8:
        blocks = [jnp.concatenate(blocks, axis=0)]
    tokens = sum(block.shape[-2] for block in blocks)
    halves = len(w_ins)
    width, hidden = w_ins[0].shape
    hidden *= halves
    extra = [gain] if paired else [in_vmem(part) for part in gates]
    weights = [in_vmem(weight) for weight in (*w_outs, *w_ins)]
    operands = [*blocks, *weights, *extra]
    return pl.pallas_call(
        functools.partial(back_kernel, len(blocks), halves, chunk, 0 if paired else None),
        out_shape=(
            shape_of((tokens // 2, width), f32),
            shape_of((tokens // 2, width), bf16),
        ),
        in_specs=[VMEM] * len(operands),
        out_specs=(VMEM, VMEM),
        compiler_params=limit(8),
        cost_estimate=pl.CostEstimate(
            flops=(6 if paired else 4) * tokens * width * hidden,
            bytes_accessed=4 * width * hidden + 2 * tokens * hidden,
            transcendentals=0,
        ),
        name="first" if paired else "back",
    )(*operands)


def fold_values(own, received, rows):
    sums = own + received.astype(f32)
    return [sums[:rows]] + [
        sums[at : at + rows].astype(bf16) for at in range(rows, sums.shape[0], rows)
    ]


def fold_kernel(rows, own, received, *outs):
    for out, value in zip(outs, fold_values(own[...], received[...], rows)):
        out[...] = value


def fold(own, received, rows):
    if rows % 8:
        return fold_values(own, received, rows)
    half, width = own.shape
    return pl.pallas_call(
        functools.partial(fold_kernel, rows),
        out_shape=tuple(
            shape_of((rows, width), bf16 if at else f32) for at in range(half // rows)
        ),
        in_specs=[VMEM] * 2,
        out_specs=tuple([VMEM] * (half // rows)),
        compiler_params=limit(2),
        name="fold",
    )(own, received)


def finish_kernel(ending, paired, x_at, tick, *refs):
    own, incoming, x_rows, gain, extra, _ = refs[:6]
    received, outs = (refs[6:-1], refs[-1:]) if ending else (refs[6:-2], refs[-2:])
    if ending:
        past, received = received[:ending], received[ending:]
    total = own[...]
    for block in received:
        total = total + block[...].astype(f32)
    inverse_rms, normed = normalised(x_rows[x_at].astype(f32))
    scaled = total * gain[...]
    inner = jnp.mean(scaled * normed, axis=-1, keepdims=True)
    incoming_rows = incoming[1] if paired else incoming[...]
    result = (incoming_rows.astype(f32) + inverse_rms * (scaled - normed * inner)).astype(bf16)
    if ending:
        for before in range(ending):
            outs[0][before, 0] = past[before][...]
        outs[0][ending, 0] = result
    else:
        outs[0][...] = result
        outs[1][...] = jnp.where(lax.axis_index("section") == 0, extra[tick], result)


def finish(own, received, incoming, x_rows, x_at, gain, fresh, tick, after, past=None):
    rows, width = own.shape
    ending = 0 if past is None else len(past)
    block = shape_of((rows, width), bf16)
    whole = shape_of((ending + 1, 1, rows, width), bf16)
    operands = [own, incoming, x_rows, gain, gain if ending else fresh, after]
    operands += (past if ending else []) + list(received)
    specs = [VMEM] * len(operands)
    specs[5] = ANY
    return pl.pallas_call(
        functools.partial(finish_kernel, ending, incoming.ndim == 3, x_at, tick),
        out_shape=whole if ending else (block, block),
        in_specs=specs,
        out_specs=VMEM if ending else (VMEM, VMEM),
        compiler_params=limit(2),
        name="finish",
    )(*operands)


def body(stash, w_in, w_out, gain, plan, arriving, fresh):
    ticks, rows = plan.shape[0], stash.shape[2]
    masks = range(2, lax.axis_size("tp"), 2)
    _, width, hidden = w_in.shape
    half = hidden // 2
    first, later = pick(plan, stash)
    moved, moved_later = from_mirror(first), from_mirror(later)
    out_a, token = load(w_out, (0, 0), (half, width), first)
    pair = pack(moved, arriving, token)
    out_b, token = load(w_out, (half, 0), (half, width), pair)
    in_a, token = load(w_in, (0, 0), (width, half), token)
    in_b, token = load(w_in, (0, half), (width, half), token)
    w_outs, w_ins = (out_a, out_b), (in_a, in_b)
    pairs = gathered(pair)
    x_later = gathered(moved_later)
    own, other = back(pairs, None, gain, w_outs, w_ins, 1024)
    incoming, x_own, x_at = pairs[0], pairs[0], 0
    results = []
    for tick in range(ticks):
        blocks = fold(own, swapped(other, 1), rows)
        received = [swapped(block, mask) for block, mask in zip(blocks[1:], masks)]
        if tick + 1 == ticks:
            return finish(
                blocks[0], received, incoming, x_own, x_at, gain, None, tick, gain, results
            )
        gates_a = gate(x_later, tick, gain, in_a, 2048, blocks[0])
        result, outgoing = finish(
            blocks[0], received, incoming, x_own, x_at, gain, fresh, tick, gates_a
        )
        results.append(result)
        gates_b = gate(x_later, tick, gain, in_b, 2048, outgoing)
        chips = [from_above(outgoing, mask) for mask in [0, *masks]]
        own, other = back(with_cores(chips), (gates_a, gates_b), gain, w_outs, w_ins, 1024)
        incoming, x_own, x_at = chips[0], x_later[0], tick


def solution(mesh):
    placed = (
        P("section", None, "tp", None),
        P("section", None, "tp"),
        P("section", "tp", None),
        P("section", None),
        P(),
        P("section", "tp", None),
        P(None, "tp", None),
    )
    return jax.shard_map(
        body, mesh=mesh, in_specs=placed, out_specs=P(None, "section", "tp", None), check_vma=False
    )
```

```python
import functools

import jax
import jax.numpy as jnp
from jax import lax
from jax.experimental import pallas as pl
from jax.experimental.pallas import tpu as pltpu
from jax.sharding import PartitionSpec as P

epsilon = 1e-06
MIB = 2**20
f32 = jnp.float32
bf16 = jnp.bfloat16
VMEM = pl.BlockSpec(memory_space=pltpu.VMEM)
HBM = pl.BlockSpec(memory_space=pltpu.HBM)
SMEM = pl.BlockSpec(memory_space=pltpu.SMEM)
ANY = pl.BlockSpec(memory_space=pl.ANY)


def shape_of(shape, dtype):
    return jax.ShapeDtypeStruct(shape, dtype)


def limit(mib):
    return pltpu.CompilerParams(vmem_limit_bytes=mib * MIB)


def in_vmem(value):
    return pltpu.with_memory_space_constraint(value, pltpu.VMEM)


def in_hbm(value):
    return pltpu.with_memory_space_constraint(value, pltpu.HBM)


def swapped(value, mask):
    return lax.ppermute(value, "tp", [(i, i ^ mask) for i in range(lax.axis_size("tp"))])


def from_mirror(value):
    count = lax.axis_size("section")
    return lax.ppermute(value, "section", [(i, (i + count // 2) % count) for i in range(count)])


def from_above(value, mask):
    sections, parts = lax.axis_size("section"), lax.axis_size("tp")
    pairs = [
        (((s + 1) % sections) * parts + (i ^ mask), s * parts + i)
        for s in range(sections)
        for i in range(parts)
    ]
    return lax.ppermute(value, ("section", "tp"), pairs)


def with_cores(chips):
    return chips + [swapped(value, 1) for value in chips]


def pick_kernel(plan, stash, picked, sems):
    sections = lax.axis_size("section")
    partner = lax.rem(lax.axis_index("section") + sections // 2, sections)
    copies = [
        pltpu.make_async_copy(stash.at[0, plan[tick, partner]], picked.at[tick], sems.at[tick])
        for tick in range(plan.shape[0])
    ]
    for copy in copies:
        copy.start()
    for copy in copies:
        copy.wait()


def pick(plan, stash):
    ticks, (_, _, rows, width) = plan.shape[0], stash.shape
    return pl.pallas_call(
        pick_kernel,
        out_shape=shape_of((ticks, rows, width), stash.dtype),
        in_specs=[SMEM, HBM],
        out_specs=VMEM,
        scratch_shapes=[pltpu.SemaphoreType.DMA((ticks,))],
        compiler_params=limit(2),
        name="pick",
    )(in_hbm(plan), in_hbm(stash))


def load_kernel(axis, weight, after, *refs):
    *halves, token, sems = refs
    copies = []
    for at, half in enumerate(halves):
        where = [slice(None), slice(None)]
        where[axis] = pl.ds(at * half.shape[axis], half.shape[axis])
        copies.append(pltpu.make_async_copy(weight.at[0, *where], half, sems.at[at]))
    for copy in copies:
        copy.start()
    token[...] = jnp.zeros_like(token)
    for copy in copies:
        copy.wait()


def load(weight, axis, after):
    shape = list(weight.shape[1:])
    shape[axis] //= 2
    half = pltpu.VMEM(tuple(shape), weight.dtype)
    *halves, token = pl.pallas_call(
        functools.partial(load_kernel, axis),
        out_shape=(half, half, shape_of((8, 128), f32)),
        in_specs=[HBM, ANY],
        out_specs=(VMEM, VMEM, VMEM),
        scratch_shapes=[pltpu.SemaphoreType.DMA((2,))],
        compiler_params=limit(2),
        cost_estimate=pl.CostEstimate(
            flops=0, bytes_accessed=8 * shape[0] * shape[1], transcendentals=0
        ),
        name="load",
    )(in_hbm(weight), after)
    return halves, token


def tie_kernel(*refs):
    pass


def tie(values, token):
    return pl.pallas_call(
        tie_kernel,
        out_shape=tuple(shape_of(value.shape, value.dtype) for value in values),
        in_specs=[ANY] * (len(values) + 1),
        out_specs=tuple([ANY] * len(values)),
        input_output_aliases={at: at for at in range(len(values))},
        compiler_params=limit(1),
        name="tie",
    )(*values, token)


def pack_kernel(many, one, after, out):
    count = many.shape[0]
    out[:count] = many[...]
    out[count] = one[0]


def pack(many, one, after):
    count, *block = many.shape
    return pl.pallas_call(
        pack_kernel,
        out_shape=shape_of((count + 1, *block), many.dtype),
        in_specs=[VMEM, VMEM, ANY],
        out_specs=VMEM,
        compiler_params=limit(2),
        name="pack",
    )(many, one, after)


def joined(blocks, at):
    return jnp.concatenate([block[at].astype(f32) for block in blocks], axis=0)


def kernel_blocks(blocks):
    if blocks[0].shape[1] % 8 == 0:
        return list(blocks)
    return [jnp.concatenate(blocks, axis=1)]


def normalised(values):
    inverse_rms = lax.rsqrt(jnp.mean(values * values, axis=-1, keepdims=True) + epsilon)
    return inverse_rms, values * inverse_rms


def gate_values(inputs, w_in, part):
    preact = jnp.dot(inputs, w_in[:, part], preferred_element_type=f32)
    return (2.0 * jnp.maximum(preact, 0.0)).T


def spans(size, chunk):
    chunk = min(chunk, size)
    return [pl.ds(at, chunk) for at in range(0, size, chunk)]


def gate_kernel(count, at, chunk, *refs):
    blocks, (gain, w_in, *_, out, token) = refs[:count], refs[count:]
    token[...] = jnp.zeros_like(token)
    inputs = (normalised(joined(blocks, at))[1] * gain[...]).astype(bf16)
    for part in spans(out.shape[0], chunk):
        out[part, :] = gate_values(inputs, w_in, part).astype(bf16)


def gate(blocks, at, gain, w_in, chunk, after, kept):
    blocks = kernel_blocks(blocks)
    tokens = sum(block.shape[1] for block in blocks)
    width, hidden = w_in.shape
    return pl.pallas_call(
        functools.partial(gate_kernel, len(blocks), at, chunk),
        out_shape=(pltpu.VMEM((hidden, tokens), bf16), shape_of((8, 128), f32)),
        in_specs=[VMEM] * (len(blocks) + 2) + [ANY] * (1 + len(kept)),
        out_specs=(VMEM, VMEM),
        compiler_params=limit(6),
        cost_estimate=pl.CostEstimate(
            flops=2 * tokens * width * hidden,
            bytes_accessed=2 * width * hidden + 2 * tokens * hidden,
            transcendentals=0,
        ),
        name="gate",
    )(*blocks, gain, in_vmem(w_in), after, *[in_vmem(value) for value in kept])


def back_kernel(count, chunk, ticks, *refs):
    blocks, (*operands, own, other) = refs[:count], refs[count:]
    w_outs, w_ins, extra = operands[:2], operands[2:4], operands[4:]
    paired = len(extra) == 1
    if paired:
        inputs = (normalised(joined(blocks, 0))[1] * extra[0][...]).astype(bf16)
    incoming = joined(blocks, ticks if paired else ...).T.astype(bf16)
    total = None
    for half, (w_out, w_in) in enumerate(zip(w_outs, w_ins)):
        for part in spans(w_out.shape[0], chunk):
            hidden_back = jnp.dot(w_out[part, :], incoming, preferred_element_type=f32)
            if paired:
                factor = gate_values(inputs, w_in, part)
            else:
                factor = extra[half][part, :].astype(f32)
            hidden_grad = (hidden_back * factor).astype(bf16)
            partial = jnp.dot(w_in[:, part], hidden_grad, preferred_element_type=f32)
            total = partial if total is None else total + partial
    sums = total.T
    rows = own.shape[0]
    own[...] = sums[:rows]
    other[...] = sums[rows:].astype(bf16)


def back(blocks, ticks, extra, w_outs, w_ins, chunk):
    paired = len(extra) == 1
    if paired:
        blocks = kernel_blocks(blocks)
    elif blocks[0].shape[0] % 8:
        blocks = [jnp.concatenate(blocks, axis=0)]
    tokens = sum(block.shape[-2] for block in blocks)
    width, hidden = w_ins[0].shape
    hidden *= 2
    extra = extra if paired else [in_vmem(part) for part in extra]
    operands = [*blocks, *[in_vmem(half) for half in (*w_outs, *w_ins)], *extra]
    return pl.pallas_call(
        functools.partial(back_kernel, len(blocks), chunk, ticks),
        out_shape=(
            shape_of((tokens // 2, width), f32),
            shape_of((tokens // 2, width), bf16),
        ),
        in_specs=[VMEM] * len(operands),
        out_specs=(VMEM, VMEM),
        compiler_params=limit(8),
        cost_estimate=pl.CostEstimate(
            flops=(6 if paired else 4) * tokens * width * hidden,
            bytes_accessed=4 * width * hidden + 2 * tokens * hidden,
            transcendentals=0,
        ),
        name="first" if paired else "back",
    )(*operands)


def fold_values(own, received, rows):
    sums = own + received.astype(f32)
    return [sums[:rows]] + [
        sums[at : at + rows].astype(bf16) for at in range(rows, sums.shape[0], rows)
    ]


def fold_kernel(rows, own, received, *outs):
    for out, value in zip(outs, fold_values(own[...], received[...], rows)):
        out[...] = value


def fold(own, received, rows):
    if rows % 8:
        return fold_values(own, received, rows)
    half, width = own.shape
    return pl.pallas_call(
        functools.partial(fold_kernel, rows),
        out_shape=tuple(
            shape_of((rows, width), bf16 if at else f32) for at in range(half // rows)
        ),
        in_specs=[VMEM] * 2,
        out_specs=tuple([VMEM] * (half // rows)),
        compiler_params=limit(2),
        name="fold",
    )(own, received)


def finish_kernel(ending, ticks, tick, *refs):
    own, incoming, x_rows, gain, extra, _ = refs[:6]
    received, outs = (refs[6:-1], refs[-1:]) if ending else (refs[6:-2], refs[-2:])
    if ending:
        past, received = received[:ending], received[ending:]
    total = own[...]
    for block in received:
        total = total + block[...].astype(f32)
    inverse_rms, normed = normalised(x_rows[tick].astype(f32))
    scaled = total * gain[...]
    inner = jnp.mean(scaled * normed, axis=-1, keepdims=True)
    incoming_rows = incoming[ticks] if ticks else incoming[...]
    result = (incoming_rows.astype(f32) + inverse_rms * (scaled - normed * inner)).astype(bf16)
    if ending:
        for before in range(ending):
            outs[0][before, 0] = past[before][...]
        outs[0][ending, 0] = result
    else:
        outs[0][...] = result
        outs[1][...] = jnp.where(lax.axis_index("section") == 0, extra[tick], result)


def finish(own, received, incoming, x_rows, gain, fresh, tick, after, past=None):
    rows, width = own.shape
    ending = 0 if past is None else len(past)
    block = shape_of((rows, width), bf16)
    whole = shape_of((ending + 1, 1, rows, width), bf16)
    operands = [own, incoming, x_rows, gain, gain if ending else fresh, after]
    operands += (past if ending else []) + list(received)
    specs = [VMEM] * len(operands)
    specs[5] = ANY
    return pl.pallas_call(
        functools.partial(
            finish_kernel, ending, x_rows.shape[0] - 1 if incoming.ndim == 3 else 0, tick
        ),
        out_shape=whole if ending else (block, block),
        in_specs=specs,
        out_specs=VMEM if ending else (VMEM, VMEM),
        compiler_params=limit(2),
        name="finish",
    )(*operands)


def body(stash, w_in, w_out, gain, plan, arriving, fresh):
    ticks, rows = plan.shape[0], stash.shape[2]
    masks = range(2, lax.axis_size("tp"), 2)
    picked = pick(plan, stash)
    moved = from_mirror(picked)
    w_outs, token = load(w_out, 0, picked)
    packed = pack(moved, arriving, token)
    chips = [swapped(packed, mask) for mask in masks]
    w_ins, token = load(w_in, 1, packed)
    gathered = with_cores([packed, *tie(chips, token)])
    own, other = back(gathered, ticks, (gain,), w_outs, w_ins, 1024)
    incoming = packed
    results = []
    for tick in range(ticks):
        blocks = fold(own, swapped(other, 1), rows)
        received = [swapped(block, mask) for block, mask in zip(blocks[1:], masks)]
        if tick + 1 == ticks:
            return finish(blocks[0], received, incoming, packed, gain, None, tick, gain, results)
        gates_a, token = gate(gathered, tick + 1, gain, w_ins[0], 2048, blocks[0], w_outs)
        result, outgoing = finish(
            blocks[0], received, incoming, packed, gain, fresh, tick, token
        )
        results.append(result)
        chips = [from_above(outgoing, mask) for mask in [0, *masks]]
        gates_b, token = gate(gathered, tick + 1, gain, w_ins[1], 2048, outgoing, w_outs)
        chips = tie(chips, token)
        incoming = chips[0]
        own, other = back(with_cores(list(chips)), ticks, (gates_a, gates_b), w_outs, w_ins, 1024)


def solution(mesh):
    placed = (
        P("section", None, "tp", None),
        P("section", None, "tp"),
        P("section", "tp", None),
        P("section", None),
        P(),
        P("section", "tp", None),
        P(None, "tp", None),
    )
    return jax.shard_map(
        body, mesh=mesh, in_specs=placed, out_specs=P(None, "section", "tp", None), check_vma=False
    )
```

```python
import functools

import jax
import jax.numpy as jnp
from jax import lax
from jax.experimental import pallas as pl
from jax.experimental.pallas import tpu as pltpu
from jax.sharding import PartitionSpec as P

epsilon = 1e-06
MIB = 2**20
f32 = jnp.float32
bf16 = jnp.bfloat16
VMEM = pl.BlockSpec(memory_space=pltpu.VMEM)
HBM = pl.BlockSpec(memory_space=pltpu.HBM)
SMEM = pl.BlockSpec(memory_space=pltpu.SMEM)
ANY = pl.BlockSpec(memory_space=pl.ANY)


def shape_of(shape, dtype):
    return jax.ShapeDtypeStruct(shape, dtype)


def limit(mib):
    return pltpu.CompilerParams(vmem_limit_bytes=mib * MIB)


def in_vmem(value):
    return pltpu.with_memory_space_constraint(value, pltpu.VMEM)


def in_hbm(value):
    return pltpu.with_memory_space_constraint(value, pltpu.HBM)


def swapped(value, mask):
    return lax.ppermute(value, "tp", [(i, i ^ mask) for i in range(lax.axis_size("tp"))])


def from_mirror(value):
    count = lax.axis_size("section")
    return lax.ppermute(value, "section", [(i, (i + count // 2) % count) for i in range(count)])


def from_above(value, mask):
    sections, parts = lax.axis_size("section"), lax.axis_size("tp")
    pairs = [
        (((s + 1) % sections) * parts + (i ^ mask), s * parts + i)
        for s in range(sections)
        for i in range(parts)
    ]
    return lax.ppermute(value, ("section", "tp"), pairs)


def with_cores(chips):
    return chips + [swapped(value, 1) for value in chips]


def pick_kernel(plan, stash, picked, sems):
    sections = lax.axis_size("section")
    partner = lax.rem(lax.axis_index("section") + sections // 2, sections)
    copies = [
        pltpu.make_async_copy(stash.at[0, plan[tick, partner]], picked.at[tick], sems.at[tick])
        for tick in range(plan.shape[0])
    ]
    for copy in copies:
        copy.start()
    for copy in copies:
        copy.wait()


def pick(plan, stash):
    ticks, (_, _, rows, width) = plan.shape[0], stash.shape
    return pl.pallas_call(
        pick_kernel,
        out_shape=shape_of((ticks, rows, width), stash.dtype),
        in_specs=[SMEM, HBM],
        out_specs=VMEM,
        scratch_shapes=[pltpu.SemaphoreType.DMA((ticks,))],
        compiler_params=limit(2),
        name="pick",
    )(in_hbm(plan), in_hbm(stash))


def load_kernel(axis, weight, after, *refs):
    *pieces, token, sems = refs
    copies = []
    for at, piece in enumerate(pieces):
        where = [slice(None), slice(None)]
        where[axis] = pl.ds(at * piece.shape[axis], piece.shape[axis])
        copies.append(pltpu.make_async_copy(weight.at[0, *where], piece, sems.at[at]))
    for copy in copies:
        copy.start()
    token[...] = jnp.zeros_like(token)
    for copy in copies:
        copy.wait()


PIECES = 4


def load(weight, axis, after):
    shape = list(weight.shape[1:])
    shape[axis] //= PIECES
    piece = pltpu.VMEM(tuple(shape), weight.dtype)
    *pieces, token = pl.pallas_call(
        functools.partial(load_kernel, axis),
        out_shape=(*[piece] * PIECES, shape_of((8, 128), f32)),
        in_specs=[HBM, ANY],
        out_specs=tuple([VMEM] * (PIECES + 1)),
        scratch_shapes=[pltpu.SemaphoreType.DMA((PIECES,))],
        compiler_params=limit(2),
        cost_estimate=pl.CostEstimate(
            flops=0, bytes_accessed=4 * PIECES * shape[0] * shape[1], transcendentals=0
        ),
        name="load",
    )(in_hbm(weight), after)
    return pieces, token


def tie_kernel(*refs):
    pass


def tie(values, token):
    return pl.pallas_call(
        tie_kernel,
        out_shape=tuple(shape_of(value.shape, value.dtype) for value in values),
        in_specs=[ANY] * (len(values) + 1),
        out_specs=tuple([ANY] * len(values)),
        input_output_aliases={at: at for at in range(len(values))},
        compiler_params=limit(1),
        name="tie",
    )(*values, token)


def pack_kernel(many, one, after, out):
    count = many.shape[0]
    out[:count] = many[...]
    out[count] = one[0]


def pack(many, one, after):
    count, *block = many.shape
    return pl.pallas_call(
        pack_kernel,
        out_shape=shape_of((count + 1, *block), many.dtype),
        in_specs=[VMEM, VMEM, ANY],
        out_specs=VMEM,
        compiler_params=limit(2),
        name="pack",
    )(many, one, after)


def joined(blocks, at):
    return jnp.concatenate([block[at].astype(f32) for block in blocks], axis=0)


def kernel_blocks(blocks):
    if blocks[0].shape[1] % 8 == 0:
        return list(blocks)
    return [jnp.concatenate(blocks, axis=1)]


def normalised(values):
    inverse_rms = lax.rsqrt(jnp.mean(values * values, axis=-1, keepdims=True) + epsilon)
    return inverse_rms, values * inverse_rms


def gate_values(inputs, w_in, part):
    preact = jnp.dot(inputs, w_in[:, part], preferred_element_type=f32)
    return (2.0 * jnp.maximum(preact, 0.0)).T


def spans(size, chunk):
    chunk = min(chunk, size)
    return [pl.ds(at, chunk) for at in range(0, size, chunk)]


def gate_kernel(count, at, pieces, chunk, *refs):
    blocks, gain, w_ins = refs[:count], refs[count], refs[count + 1 : count + 1 + pieces]
    *outs, token = refs[-pieces - 1 :]
    token[...] = jnp.zeros_like(token)
    inputs = (normalised(joined(blocks, at))[1] * gain[...]).astype(bf16)
    chunk = min(chunk, outs[0].shape[0])
    for w_in, out in zip(w_ins, outs):

        def step(at, _, w_in=w_in, out=out):
            part = pl.ds(pl.multiple_of(at * chunk, chunk), chunk)
            out[part, :] = gate_values(inputs, w_in, part).astype(bf16)
            return 0

        lax.fori_loop(0, out.shape[0] // chunk, step, 0)


def gate(blocks, at, gain, w_ins, chunk, after, kept):
    blocks = kernel_blocks(blocks)
    tokens = sum(block.shape[1] for block in blocks)
    width, hidden = w_ins[0].shape
    pieces = len(w_ins)
    w_ins, kept = [[in_vmem(value) for value in values] for values in (w_ins, kept)]
    *gates, token = pl.pallas_call(
        functools.partial(gate_kernel, len(blocks), at, pieces, chunk),
        out_shape=(*[pltpu.VMEM((hidden, tokens), bf16)] * pieces, shape_of((8, 128), f32)),
        in_specs=[VMEM] * (len(blocks) + 1 + pieces) + [ANY] * (1 + len(kept)),
        out_specs=tuple([VMEM] * (pieces + 1)),
        compiler_params=limit(4),
        cost_estimate=pl.CostEstimate(
            flops=2 * tokens * width * hidden * pieces,
            bytes_accessed=(2 * width + 2 * tokens) * hidden * pieces,
            transcendentals=0,
        ),
        name="gate",
    )(*blocks, gain, *w_ins, after, *kept)
    return gates, token


def back_kernel(count, chunk, ticks, *refs):
    blocks, (*operands, own, other) = refs[:count], refs[count:]
    w_outs, w_ins, extra = operands[:PIECES], operands[PIECES : 2 * PIECES], operands[2 * PIECES :]
    paired = len(extra) == 1
    if paired:
        inputs = (normalised(joined(blocks, 0))[1] * extra[0][...]).astype(bf16)
    incoming = joined(blocks, ticks if paired else ...).T.astype(bf16)
    total = None
    for half, (w_out, w_in) in enumerate(zip(w_outs, w_ins)):
        for part in spans(w_out.shape[0], chunk):
            hidden_back = jnp.dot(w_out[part, :], incoming, preferred_element_type=f32)
            if paired:
                factor = gate_values(inputs, w_in, part)
            else:
                factor = extra[half][part, :].astype(f32)
            hidden_grad = (hidden_back * factor).astype(bf16)
            partial = jnp.dot(w_in[:, part], hidden_grad, preferred_element_type=f32)
            total = partial if total is None else total + partial
    sums = total.T
    rows = own.shape[0]
    own[...] = sums[:rows]
    other[...] = sums[rows:].astype(bf16)


def back(blocks, ticks, extra, w_outs, w_ins, chunk):
    paired = len(extra) == 1
    if paired:
        blocks = kernel_blocks(blocks)
    elif blocks[0].shape[0] % 8:
        blocks = [jnp.concatenate(blocks, axis=0)]
    tokens = sum(block.shape[-2] for block in blocks)
    width, hidden = w_ins[0].shape
    hidden *= PIECES
    extra = extra if paired else [in_vmem(part) for part in extra]
    operands = [*blocks, *[in_vmem(half) for half in (*w_outs, *w_ins)], *extra]
    return pl.pallas_call(
        functools.partial(back_kernel, len(blocks), chunk, ticks),
        out_shape=(
            shape_of((tokens // 2, width), f32),
            shape_of((tokens // 2, width), bf16),
        ),
        in_specs=[VMEM] * len(operands),
        out_specs=(VMEM, VMEM),
        compiler_params=limit(8 if paired else 6),
        cost_estimate=pl.CostEstimate(
            flops=(6 if paired else 4) * tokens * width * hidden,
            bytes_accessed=4 * width * hidden + 2 * tokens * hidden,
            transcendentals=0,
        ),
        name="first" if paired else "back",
    )(*operands)


def fold_values(own, received, rows):
    sums = own + received.astype(f32)
    return [sums[:rows]] + [
        sums[at : at + rows].astype(bf16) for at in range(rows, sums.shape[0], rows)
    ]


def fold_kernel(rows, own, received, *outs):
    for out, value in zip(outs, fold_values(own[...], received[...], rows)):
        out[...] = value


def fold(own, received, rows):
    if rows % 8:
        return fold_values(own, received, rows)
    half, width = own.shape
    return pl.pallas_call(
        functools.partial(fold_kernel, rows),
        out_shape=tuple(
            shape_of((rows, width), bf16 if at else f32) for at in range(half // rows)
        ),
        in_specs=[VMEM] * 2,
        out_specs=tuple([VMEM] * (half // rows)),
        compiler_params=limit(2),
        name="fold",
    )(own, received)


def finish_kernel(ending, ticks, tick, *refs):
    own, incoming, x_rows, gain, extra, _ = refs[:6]
    received, outs = (refs[6:-1], refs[-1:]) if ending else (refs[6:-2], refs[-2:])
    if ending:
        past, received = received[:ending], received[ending:]
    total = own[...]
    for block in received:
        total = total + block[...].astype(f32)
    inverse_rms, normed = normalised(x_rows[tick].astype(f32))
    scaled = total * gain[...]
    inner = jnp.mean(scaled * normed, axis=-1, keepdims=True)
    incoming_rows = incoming[ticks] if ticks else incoming[...]
    result = (incoming_rows.astype(f32) + inverse_rms * (scaled - normed * inner)).astype(bf16)
    if ending:
        for before in range(ending):
            outs[0][before, 0] = past[before][...]
        outs[0][ending, 0] = result
    else:
        outs[0][...] = result
        outs[1][...] = jnp.where(lax.axis_index("section") == 0, extra[tick], result)


def finish(own, received, incoming, x_rows, gain, fresh, tick, after, past=None):
    rows, width = own.shape
    ending = 0 if past is None else len(past)
    block = shape_of((rows, width), bf16)
    whole = shape_of((ending + 1, 1, rows, width), bf16)
    operands = [own, incoming, x_rows, gain, gain if ending else fresh, after]
    operands += (past if ending else []) + list(received)
    specs = [VMEM] * len(operands)
    specs[5] = ANY
    return pl.pallas_call(
        functools.partial(
            finish_kernel, ending, x_rows.shape[0] - 1 if incoming.ndim == 3 else 0, tick
        ),
        out_shape=whole if ending else (block, block),
        in_specs=specs,
        out_specs=VMEM if ending else (VMEM, VMEM),
        compiler_params=limit(2),
        name="finish",
    )(*operands)


def body(stash, w_in, w_out, gain, plan, arriving, fresh):
    ticks, rows = plan.shape[0], stash.shape[2]
    masks = range(2, lax.axis_size("tp"), 2)
    picked = pick(plan, stash)
    moved = from_mirror(picked)
    w_outs, token = load(w_out, 0, picked)
    packed = pack(moved, arriving, token)
    chips = [swapped(packed, mask) for mask in masks]
    w_ins, token = load(w_in, 1, packed)
    gathered = with_cores([packed, *tie(chips, token)])
    own, other = back(gathered, ticks, (gain,), w_outs, w_ins, 1024)
    incoming = packed
    results = []
    for tick in range(ticks):
        blocks = fold(own, swapped(other, 1), rows)
        received = [swapped(block, mask) for block, mask in zip(blocks[1:], masks)]
        if tick + 1 == ticks:
            return finish(blocks[0], received, incoming, packed, gain, None, tick, gain, results)
        half = PIECES // 2
        gates_a, token = gate(gathered, tick + 1, gain, w_ins[:half], 1024, blocks[0], w_outs)
        result, outgoing = finish(
            blocks[0], received, incoming, packed, gain, fresh, tick, token
        )
        results.append(result)
        chips = [from_above(outgoing, mask) for mask in [0, *masks]]
        gates_b, token = gate(gathered, tick + 1, gain, w_ins[half:], 1024, outgoing, w_outs)
        chips = tie(chips, token)
        incoming = chips[0]
        own, other = back(with_cores(list(chips)), ticks, (*gates_a, *gates_b), w_outs, w_ins, 1024)


def solution(mesh):
    placed = (
        P("section", None, "tp", None),
        P("section", None, "tp"),
        P("section", "tp", None),
        P("section", None),
        P(),
        P("section", "tp", None),
        P(None, "tp", None),
    )
    return jax.shard_map(
        body, mesh=mesh, in_specs=placed, out_specs=P(None, "section", "tp", None), check_vma=False
    )
```

```python
import functools

import jax
import jax.numpy as jnp
from jax import lax
from jax.experimental import pallas as pl
from jax.experimental.pallas import tpu as pltpu
from jax.sharding import PartitionSpec as P

epsilon = 1e-06
MIB = 2**20
f32 = jnp.float32
bf16 = jnp.bfloat16
VMEM = pl.BlockSpec(memory_space=pltpu.VMEM)
HBM = pl.BlockSpec(memory_space=pltpu.HBM)
SMEM = pl.BlockSpec(memory_space=pltpu.SMEM)
ANY = pl.BlockSpec(memory_space=pl.ANY)


def shape_of(shape, dtype):
    return jax.ShapeDtypeStruct(shape, dtype)


def limit(mib):
    return pltpu.CompilerParams(vmem_limit_bytes=mib * MIB)


def in_vmem(value):
    return pltpu.with_memory_space_constraint(value, pltpu.VMEM)


def in_hbm(value):
    return pltpu.with_memory_space_constraint(value, pltpu.HBM)


def swapped(value, mask):
    return lax.ppermute(value, "tp", [(i, i ^ mask) for i in range(lax.axis_size("tp"))])


def from_mirror(value):
    count = lax.axis_size("section")
    return lax.ppermute(value, "section", [(i, (i + count // 2) % count) for i in range(count)])


def from_above(value, mask):
    sections, parts = lax.axis_size("section"), lax.axis_size("tp")
    pairs = [
        (((s + 1) % sections) * parts + (i ^ mask), s * parts + i)
        for s in range(sections)
        for i in range(parts)
    ]
    return lax.ppermute(value, ("section", "tp"), pairs)


def with_cores(chips):
    return chips + [swapped(value, 1) for value in chips]


def pick_kernel(plan, stash, picked, sems):
    sections = lax.axis_size("section")
    partner = lax.rem(lax.axis_index("section") + sections // 2, sections)
    copies = [
        pltpu.make_async_copy(stash.at[0, plan[tick, partner]], picked.at[tick], sems.at[tick])
        for tick in range(plan.shape[0])
    ]
    for copy in copies:
        copy.start()
    for copy in copies:
        copy.wait()


def pick(plan, stash):
    ticks, (_, _, rows, width) = plan.shape[0], stash.shape
    return pl.pallas_call(
        pick_kernel,
        out_shape=shape_of((ticks, rows, width), stash.dtype),
        in_specs=[SMEM, HBM],
        out_specs=VMEM,
        scratch_shapes=[pltpu.SemaphoreType.DMA((ticks,))],
        compiler_params=limit(6),
        name="pick",
    )(in_hbm(plan), in_hbm(stash))


def load_kernel(axis, weight, after, *refs):
    *pieces, token, sems = refs
    copies = []
    for at, piece in enumerate(pieces):
        where = [slice(None), slice(None)]
        where[axis] = pl.ds(at * piece.shape[axis], piece.shape[axis])
        copies.append(pltpu.make_async_copy(weight.at[0, *where], piece, sems.at[at]))
    for copy in copies:
        copy.start()
    token[...] = jnp.zeros_like(token)
    for copy in copies:
        copy.wait()


PIECES = 8


def load(weight, axis, after):
    shape = list(weight.shape[1:])
    shape[axis] //= PIECES
    piece = pltpu.VMEM(tuple(shape), weight.dtype)
    *pieces, token = pl.pallas_call(
        functools.partial(load_kernel, axis),
        out_shape=(*[piece] * PIECES, shape_of((8, 128), f32)),
        in_specs=[HBM, ANY],
        out_specs=tuple([VMEM] * (PIECES + 1)),
        scratch_shapes=[pltpu.SemaphoreType.DMA((PIECES,))],
        compiler_params=limit(6),
        cost_estimate=pl.CostEstimate(
            flops=0, bytes_accessed=4 * PIECES * shape[0] * shape[1], transcendentals=0
        ),
        name="load",
    )(in_hbm(weight), after)
    return pieces, token


def tie_kernel(*refs):
    pass


def tie(values, token):
    return pl.pallas_call(
        tie_kernel,
        out_shape=tuple(shape_of(value.shape, value.dtype) for value in values),
        in_specs=[ANY] * (len(values) + 1),
        out_specs=tuple([ANY] * len(values)),
        input_output_aliases={at: at for at in range(len(values))},
        compiler_params=limit(1),
        name="tie",
    )(*values, token)


def pack_kernel(many, one, after, out):
    count = many.shape[0]
    out[:count] = many[...]
    out[count] = one[0]


def pack(many, one, after):
    count, *block = many.shape
    return pl.pallas_call(
        pack_kernel,
        out_shape=shape_of((count + 1, *block), many.dtype),
        in_specs=[VMEM, VMEM, ANY],
        out_specs=VMEM,
        compiler_params=limit(6),
        name="pack",
    )(many, one, after)


def joined(blocks, at):
    return jnp.concatenate([block[at].astype(f32) for block in blocks], axis=0)


def joined_pairs(blocks):
    return jnp.concatenate([block[at].astype(f32) for block in blocks for at in (0, 1)], axis=0)


def kernel_blocks(blocks):
    if blocks[0].shape[1] % 8 == 0:
        return list(blocks)
    return [jnp.concatenate(blocks, axis=1)]


def normalised(values):
    inverse_rms = lax.rsqrt(jnp.mean(values * values, axis=-1, keepdims=True) + epsilon)
    return inverse_rms, values * inverse_rms


def gate_values(inputs, w_in, part):
    preact = jnp.dot(inputs, w_in[:, part], preferred_element_type=f32)
    return (2.0 * jnp.maximum(preact, 0.0)).T


def spans(size, chunk):
    chunk = min(chunk, size)
    return [pl.ds(at, chunk) for at in range(0, size, chunk)]


def gate_kernel(count, at, pieces, chunk, *refs):
    blocks, gain, w_ins = refs[:count], refs[count], refs[count + 1 : count + 1 + pieces]
    *outs, token = refs[-pieces - 1 :]
    token[...] = jnp.zeros_like(token)
    inputs = (normalised(joined(blocks, at))[1] * gain[...]).astype(bf16)
    chunk = min(chunk, outs[0].shape[0])
    for w_in, out in zip(w_ins, outs):

        def step(at, _, w_in=w_in, out=out):
            part = pl.ds(pl.multiple_of(at * chunk, chunk), chunk)
            out[part, :] = gate_values(inputs, w_in, part).astype(bf16)
            return 0

        lax.fori_loop(0, out.shape[0] // chunk, step, 0)


def gate(blocks, at, gain, w_ins, chunk, after, kept):
    blocks = kernel_blocks(blocks)
    tokens = sum(block.shape[1] for block in blocks)
    width, hidden = w_ins[0].shape
    pieces = len(w_ins)
    w_ins, kept = [[in_vmem(value) for value in values] for values in (w_ins, kept)]
    *gates, token = pl.pallas_call(
        functools.partial(gate_kernel, len(blocks), at, pieces, chunk),
        out_shape=(*[pltpu.VMEM((hidden, tokens), bf16)] * pieces, shape_of((8, 128), f32)),
        in_specs=[VMEM] * (len(blocks) + 1 + pieces) + [ANY] * (1 + len(kept)),
        out_specs=tuple([VMEM] * (pieces + 1)),
        compiler_params=limit(6),
        cost_estimate=pl.CostEstimate(
            flops=2 * tokens * width * hidden * pieces,
            bytes_accessed=(2 * width + 2 * tokens) * hidden * pieces,
            transcendentals=0,
        ),
        name="gate",
    )(*blocks, gain, *w_ins, after, *kept)
    return gates, token


def back_kernel(count, chunk, ticks, *refs):
    blocks, (*operands, own, other) = refs[:count], refs[count:]
    w_outs, w_ins, extra = operands[:PIECES], operands[PIECES : 2 * PIECES], operands[2 * PIECES :]
    paired = len(extra) == 1
    if paired:
        inputs = (normalised(joined(blocks, 0))[1] * extra[0][...]).astype(bf16)
    incoming = joined(blocks, ticks) if paired else joined_pairs(blocks)
    incoming = incoming.T.astype(bf16)
    total = None
    for half, (w_out, w_in) in enumerate(zip(w_outs, w_ins)):
        for part in spans(w_out.shape[0], chunk):
            hidden_back = jnp.dot(w_out[part, :], incoming, preferred_element_type=f32)
            if paired:
                factor = gate_values(inputs, w_in, part)
            else:
                factor = extra[half][part, :].astype(f32)
            hidden_grad = (hidden_back * factor).astype(bf16)
            partial = jnp.dot(w_in[:, part], hidden_grad, preferred_element_type=f32)
            total = partial if total is None else total + partial
    sums = total.T
    rows = own.shape[0]
    own[...] = sums[:rows]
    other[...] = sums[rows:].astype(bf16)


def back(blocks, ticks, extra, w_outs, w_ins, chunk):
    paired = len(extra) == 1
    if paired:
        blocks = kernel_blocks(blocks)
    elif blocks[0].shape[1] % 8:
        blocks = [joined_pairs(blocks).astype(bf16).reshape(2, -1, blocks[0].shape[2])]
    tokens = sum(block.shape[-2] for block in blocks) * (1 if paired else 2)
    width, hidden = w_ins[0].shape
    hidden *= PIECES
    extra = extra if paired else [in_vmem(part) for part in extra]
    operands = [*blocks, *[in_vmem(half) for half in (*w_outs, *w_ins)], *extra]
    return pl.pallas_call(
        functools.partial(back_kernel, len(blocks), chunk, ticks),
        out_shape=(
            shape_of((tokens // 2, width), f32),
            shape_of((tokens // 2, width), bf16),
        ),
        in_specs=[VMEM] * len(operands),
        out_specs=(VMEM, VMEM),
        compiler_params=limit(6),
        cost_estimate=pl.CostEstimate(
            flops=(6 if paired else 4) * tokens * width * hidden,
            bytes_accessed=4 * width * hidden + 2 * tokens * hidden,
            transcendentals=0,
        ),
        name="first" if paired else "back",
    )(*operands)


def fold_values(own, received, rows, near):
    sums = own + received.astype(f32)
    blocks = [sums[at : at + rows] for at in range(0, sums.shape[0], rows)]
    if not near:
        return blocks[:1] + [block.astype(bf16) for block in blocks[1:]]
    pairs = [jnp.stack([blocks[at], blocks[at ^ 1]]) for at in range(len(blocks))]
    return pairs[:1] + [pair.astype(bf16) for pair in pairs[1:]]


def fold_kernel(rows, near, own, received, *outs):
    for out, value in zip(outs, fold_values(own[...], received[...], rows, near)):
        out[...] = value


def fold(own, received, rows, near):
    if rows % 8:
        return fold_values(own, received, rows, near)
    half, width = own.shape
    shape = (2, rows, width) if near else (rows, width)
    return pl.pallas_call(
        functools.partial(fold_kernel, rows, near),
        out_shape=tuple(shape_of(shape, bf16 if at else f32) for at in range(half // rows)),
        in_specs=[VMEM] * 2,
        out_specs=tuple([VMEM] * (half // rows)),
        compiler_params=limit(6),
        name="fold",
    )(own, received)


def finished(own, received, incoming, x_rows, gain):
    total = own
    for block in received:
        total = total + block.astype(f32)
    inverse_rms, normed = normalised(x_rows.astype(f32))
    scaled = total * gain
    inner = jnp.mean(scaled * normed, axis=-1, keepdims=True)
    return (incoming.astype(f32) + inverse_rms * (scaled - normed * inner)).astype(bf16)


def finish_kernel(count, tick, paired, x_own, x_near, gain, fresh, fresh_near, *refs):
    (incoming, own, *received), (_, result, outgoing) = refs[:count], refs[count:]
    for at, (x_rows, extra) in enumerate(((x_own, fresh), (x_near, fresh_near))):
        rows = (x_own, x_near)[at][x_own.shape[0] - 1] if paired else incoming[at]
        value = finished(
            own[at], [block[at] for block in received], rows, x_rows[tick], gain[...]
        )
        if at == 0:
            result[...] = value
        outgoing[at] = jnp.where(lax.axis_index("section") == 0, extra[tick], value)


def finish(own, received, incoming, gathered, gain, fresh, fresh_near, tick, after):
    pair, rows, width = own.shape
    paired = incoming.ndim == 3 and incoming.shape[0] != pair
    operands = [gathered[0], gathered[1], gain, fresh, fresh_near, incoming, own, *received]
    return pl.pallas_call(
        functools.partial(finish_kernel, 2 + len(received), tick, paired),
        out_shape=(shape_of((rows, width), bf16), shape_of((pair, rows, width), bf16)),
        in_specs=[VMEM] * len(operands) + [ANY],
        out_specs=(VMEM, VMEM),
        compiler_params=limit(6),
        name="finish",
    )(*operands, after)


def end_kernel(count, x_own, gain, incoming, own, *refs):
    received, (*past, out) = refs[:count], refs[count:]
    for before, value in enumerate(past):
        out[before, 0] = value[...]
    received = [block[...] for block in received]
    out[len(past), 0] = finished(
        own[...], received, incoming[0], x_own[len(past)], gain[...]
    )


def end(own, received, incoming, x_own, gain, past):
    operands = [x_own, gain, incoming, own, *received, *past]
    return pl.pallas_call(
        functools.partial(end_kernel, len(received)),
        out_shape=shape_of((len(past) + 1, 1, *own.shape), bf16),
        in_specs=[VMEM] * len(operands),
        out_specs=VMEM,
        compiler_params=limit(6),
        name="end",
    )(*operands)


def body(stash, w_in, w_out, gain, plan, arriving, fresh):
    ticks, rows = plan.shape[0], stash.shape[2]
    parts = lax.axis_size("tp")
    masks = range(2, parts, 2)
    picked = pick(plan, stash)
    moved = from_mirror(picked)
    w_outs, token = load(w_out, 0, picked)
    packed = pack(moved, arriving, token)
    chips = [swapped(packed, mask) for mask in masks]
    w_ins, token = load(w_in, 1, packed)
    gathered = with_cores([packed, *tie(chips, token)])
    fresh_near = swapped(fresh, 2)
    own, other = back(gathered, ticks, (gain,), w_outs, w_ins, 512)
    incoming = packed
    results = []
    for tick in range(ticks):
        last = tick + 1 == ticks
        blocks = fold(own, swapped(other, 1), rows, not last)
        received = [swapped(block, mask) for block, mask in zip(blocks[1:], masks)]
        if last:
            return end(blocks[0], received, incoming, packed, gain, results)
        half = PIECES // 2
        gates_a, token = gate(gathered, tick + 1, gain, w_ins[:half], 1024, blocks[0], w_outs)
        result, outgoing = finish(
            blocks[0], received, incoming, gathered, gain, fresh, fresh_near, tick, token
        )
        results.append(result)
        came = [from_above(outgoing, mask) for mask in range(0, parts, 4)]
        gates_b, token = gate(gathered, tick + 1, gain, w_ins[half:], 1024, outgoing, w_outs)
        halves = with_cores(list(tie(came, token)))
        incoming = halves[0]
        own, other = back(halves, ticks, (*gates_a, *gates_b), w_outs, w_ins, 512)


def solution(mesh):
    placed = (
        P("section", None, "tp", None),
        P("section", None, "tp"),
        P("section", "tp", None),
        P("section", None),
        P(),
        P("section", "tp", None),
        P(None, "tp", None),
    )
    return jax.shard_map(
        body, mesh=mesh, in_specs=placed, out_specs=P(None, "section", "tp", None), check_vma=False
    )
```

```python
import functools

import jax
import jax.numpy as jnp
from jax import lax
from jax.experimental import pallas as pl
from jax.experimental.pallas import tpu as pltpu
from jax.sharding import PartitionSpec as P

epsilon = 1e-06
MIB = 2**20
f32 = jnp.float32
bf16 = jnp.bfloat16
VMEM = pl.BlockSpec(memory_space=pltpu.VMEM)
HBM = pl.BlockSpec(memory_space=pltpu.HBM)
SMEM = pl.BlockSpec(memory_space=pltpu.SMEM)
ANY = pl.BlockSpec(memory_space=pl.ANY)


def shape_of(shape, dtype):
    return jax.ShapeDtypeStruct(shape, dtype)


def limit(mib):
    return pltpu.CompilerParams(vmem_limit_bytes=mib * MIB)


def in_vmem(value):
    return pltpu.with_memory_space_constraint(value, pltpu.VMEM)


def in_hbm(value):
    return pltpu.with_memory_space_constraint(value, pltpu.HBM)


def swapped(value, mask):
    return lax.ppermute(value, "tp", [(i, i ^ mask) for i in range(lax.axis_size("tp"))])


def from_mirror(value):
    count = lax.axis_size("section")
    return lax.ppermute(value, "section", [(i, (i + count // 2) % count) for i in range(count)])


def from_above(value, mask):
    sections, parts = lax.axis_size("section"), lax.axis_size("tp")
    pairs = [
        (((s + 1) % sections) * parts + (i ^ mask), s * parts + i)
        for s in range(sections)
        for i in range(parts)
    ]
    return lax.ppermute(value, ("section", "tp"), pairs)


def with_cores(chips):
    return chips + [swapped(value, 1) for value in chips]


def pick_kernel(plan, stash, first, later, slots, stored, sems):
    sections = lax.axis_size("section")
    partner = lax.rem(lax.axis_index("section") + sections // 2, sections)
    copies = [
        pltpu.make_async_copy(plan, slots, sems.at[0]),
        pltpu.make_async_copy(stash.at[0], stored, sems.at[1]),
    ]
    for copy in copies:
        copy.start()
    for copy in copies:
        copy.wait()
    first[...] = stored[slots[0, partner]]
    for tick in range(later.shape[1]):
        later[0, tick] = stored[slots[tick + 1, partner]]


def pick(plan, stash):
    ticks, (_, _, rows, width) = plan.shape[0], stash.shape
    return pl.pallas_call(
        pick_kernel,
        out_shape=(
            shape_of((rows, width), stash.dtype),
            shape_of((1, ticks - 1, rows, width), stash.dtype),
        ),
        in_specs=[HBM, HBM],
        out_specs=(VMEM, VMEM),
        scratch_shapes=[
            pltpu.SMEM(plan.shape, plan.dtype),
            pltpu.VMEM(stash.shape[1:], stash.dtype),
            pltpu.SemaphoreType.DMA((2,)),
        ],
        compiler_params=limit(6),
        name="pick",
    )(in_hbm(plan), in_hbm(stash))


PIECES = 8
FIRST, SECOND = 4, 10


def piece_copies(wanted, weights, outs, sems):
    copies = []
    for at, ((which, piece), out) in enumerate(zip(wanted, outs)):
        where = [slice(None), slice(None)]
        axis = 1 - which
        where[axis] = pl.ds(piece * out.shape[axis], out.shape[axis])
        copies.append(pltpu.make_async_copy(weights[which].at[0, *where], out, sems.at[at]))
    return copies


def piece_shapes(wanted, weights):
    shapes = []
    for which, _ in wanted:
        shape = list(weights[which].shape[1:])
        shape[1 - which] //= PIECES
        shapes.append(pltpu.VMEM(tuple(shape), weights[which].dtype))
    return shapes


def load_kernel(wanted, w_in, w_out, after, *refs):
    *outs, token, sems = refs
    copies = piece_copies(wanted, (w_in, w_out), outs, sems)
    for copy in copies:
        copy.start()
    token[...] = jnp.zeros_like(token)
    for copy in copies:
        copy.wait()


def load(weights, wanted, after):
    shapes = piece_shapes(wanted, weights)
    *pieces, token = pl.pallas_call(
        functools.partial(load_kernel, wanted),
        out_shape=(*shapes, shape_of((8, 128), f32)),
        in_specs=[HBM, HBM, ANY],
        out_specs=tuple([VMEM] * (len(wanted) + 1)),
        scratch_shapes=[pltpu.SemaphoreType.DMA((len(wanted),))],
        compiler_params=limit(6),
        cost_estimate=pl.CostEstimate(
            flops=0,
            bytes_accessed=4 * sum(shape.shape[0] * shape.shape[1] for shape in shapes),
            transcendentals=0,
        ),
        name="load",
    )(*[in_hbm(weight) for weight in weights], after)
    return pieces, token


def tie_kernel(*refs):
    pass


def tie(values, token):
    return pl.pallas_call(
        tie_kernel,
        out_shape=tuple(shape_of(value.shape, value.dtype) for value in values),
        in_specs=[ANY] * (len(values) + 1),
        out_specs=tuple([ANY] * len(values)),
        input_output_aliases={at: at for at in range(len(values))},
        compiler_params=limit(1),
        name="tie",
    )(*values, token)


def pack_kernel(one, other, after, out):
    out[0] = one[...]
    out[1] = other[0]


def pack(one, other, after):
    return pl.pallas_call(
        pack_kernel,
        out_shape=shape_of((2, *one.shape), one.dtype),
        in_specs=[VMEM, VMEM, ANY],
        out_specs=VMEM,
        compiler_params=limit(6),
        name="pack",
    )(one, other, after)


def double_kernel(one, other, after, out):
    count = one.shape[0]
    out[:count] = one[...]
    out[count:] = other[...]


def double(one, other, after):
    count, *block = one.shape
    return pl.pallas_call(
        double_kernel,
        out_shape=shape_of((2 * count, *block), one.dtype),
        in_specs=[VMEM, VMEM, ANY],
        out_specs=VMEM,
        compiler_params=limit(6),
        name="double",
    )(one, other, after)


def joined(blocks, places):
    return jnp.concatenate([blocks[block][at].astype(f32) for block, at in places], axis=0)


def for_kernel(blocks, places):
    if blocks[0].shape[-2] % 8 == 0:
        return list(blocks), places
    return [joined(blocks, places).astype(bf16)], [(0, ...)]


def normalised(values):
    inverse_rms = lax.rsqrt(jnp.mean(values * values, axis=-1, keepdims=True) + epsilon)
    return inverse_rms, values * inverse_rms


def gate_values(inputs, w_in, part):
    preact = jnp.dot(inputs, w_in[:, part], preferred_element_type=f32)
    return (2.0 * jnp.maximum(preact, 0.0)).T


def spans(size, chunk):
    chunk = min(chunk, size)
    return [pl.ds(at, chunk) for at in range(0, size, chunk)]


def gate_kernel(places, counts, wanted, chunk, *refs):
    blocks, refs = refs[: counts[0]], refs[counts[0] :]
    gain, w_ins, refs = refs[0], refs[1 : 1 + counts[1]], refs[1 + counts[1] :]
    weights, refs = refs[:2], refs[2 + counts[2] :]
    gates, outs, (token, sems) = refs[: counts[1]], refs[counts[1] : -2], refs[-2:]
    copies = piece_copies(wanted, weights, outs, sems)
    for copy in copies:
        copy.start()
    token[...] = jnp.zeros_like(token)
    inputs = (normalised(joined(blocks, places))[1] * gain[...]).astype(bf16)
    for w_in, out in zip(w_ins, gates):
        for part in spans(out.shape[0], chunk):
            out[part, :] = gate_values(inputs, w_in, part).astype(bf16)
    for copy in copies:
        copy.wait()


def gate(blocks, places, gain, w_ins, chunk, weights, wanted, after):
    blocks, places = for_kernel(blocks, places)
    tokens = sum(block.shape[-2] for block in blocks) if places == [(0, ...)] else None
    if tokens is None:
        tokens = len(places) * blocks[0].shape[-2]
    width, hidden = w_ins[0].shape
    count = len(w_ins)
    *outs, token = pl.pallas_call(
        functools.partial(gate_kernel, places, (len(blocks), count, len(after)), wanted, chunk),
        out_shape=(
            *[pltpu.VMEM((hidden, tokens), bf16)] * count,
            *piece_shapes(wanted, weights),
            shape_of((8, 128), f32),
        ),
        in_specs=[VMEM] * (len(blocks) + 1 + count) + [HBM] * 2 + [ANY] * len(after),
        out_specs=tuple([VMEM] * (count + len(wanted) + 1)),
        scratch_shapes=[pltpu.SemaphoreType.DMA((max(len(wanted), 1),))],
        compiler_params=limit(6),
        cost_estimate=pl.CostEstimate(
            flops=2 * tokens * width * hidden * count,
            bytes_accessed=(2 * width + 2 * tokens) * hidden * count,
            transcendentals=0,
        ),
        name="gate",
    )(
        *blocks,
        gain,
        *[in_vmem(piece) for piece in w_ins],
        *[in_hbm(weight) for weight in weights],
        *after,
    )
    return outs[:count], outs[count:], token


def back_kernel(places, count, chunk, *refs):
    blocks, (*operands, own, other) = refs[:count], refs[count:]
    w_outs, w_ins, gates = [operands[at : at + PIECES] for at in range(0, 3 * PIECES, PIECES)]
    incoming = joined(blocks, places).T.astype(bf16)
    total = None
    for w_out, w_in, gate_piece in zip(w_outs, w_ins, gates):
        for part in spans(w_out.shape[0], chunk):
            hidden_back = jnp.dot(w_out[part, :], incoming, preferred_element_type=f32)
            hidden_grad = (hidden_back * gate_piece[part, :].astype(f32)).astype(bf16)
            partial = jnp.dot(w_in[:, part], hidden_grad, preferred_element_type=f32)
            total = partial if total is None else total + partial
    sums = total.T
    rows = own.shape[0]
    own[...] = sums[:rows]
    other[...] = sums[rows:].astype(bf16)


def back(blocks, places, gates, w_outs, w_ins, chunk):
    blocks, places = for_kernel(blocks, places)
    tokens = gates[0].shape[1]
    width, hidden = w_ins[0].shape
    hidden *= PIECES
    operands = [*blocks, *[in_vmem(piece) for piece in (*w_outs, *w_ins, *gates)]]
    return pl.pallas_call(
        functools.partial(back_kernel, places, len(blocks), chunk),
        out_shape=(
            shape_of((tokens // 2, width), f32),
            shape_of((tokens // 2, width), bf16),
        ),
        in_specs=[VMEM] * len(operands),
        out_specs=(VMEM, VMEM),
        compiler_params=limit(6),
        cost_estimate=pl.CostEstimate(
            flops=4 * tokens * width * hidden,
            bytes_accessed=4 * width * hidden + 2 * tokens * hidden,
            transcendentals=0,
        ),
        name="back",
    )(*operands)


def fold_values(own, received, rows, near):
    sums = own + received.astype(f32)
    blocks = [sums[at : at + rows] for at in range(0, sums.shape[0], rows)]
    if not near:
        return blocks[:1] + [block.astype(bf16) for block in blocks[1:]]
    pairs = [jnp.stack([blocks[at], blocks[at ^ 1]]) for at in range(len(blocks))]
    return pairs[:1] + [pair.astype(bf16) for pair in pairs[1:]]


def fold_kernel(rows, near, own, received, *outs):
    for out, value in zip(outs, fold_values(own[...], received[...], rows, near)):
        out[...] = value


def fold(own, received, rows, near):
    if rows % 8:
        return fold_values(own, received, rows, near)
    half, width = own.shape
    shape = (2, rows, width) if near else (rows, width)
    return pl.pallas_call(
        functools.partial(fold_kernel, rows, near),
        out_shape=tuple(shape_of(shape, bf16 if at else f32) for at in range(half // rows)),
        in_specs=[VMEM] * 2,
        out_specs=tuple([VMEM] * (half // rows)),
        compiler_params=limit(6),
        name="fold",
    )(own, received)


def finished(own, received, incoming, x_rows, gain):
    total = own
    for block in received:
        total = total + block.astype(f32)
    inverse_rms, normed = normalised(x_rows.astype(f32))
    scaled = total * gain
    inner = jnp.mean(scaled * normed, axis=-1, keepdims=True)
    return (incoming.astype(f32) + inverse_rms * (scaled - normed * inner)).astype(bf16)


def finish_kernel(places, count, tick, gain, fresh, fresh_near, *refs):
    blocks, refs = refs[: count[0]], refs[count[0] :]
    own, received, (_, result, outgoing) = refs[0], refs[1 : count[1]], refs[count[1] :]
    for at, extra in enumerate((fresh, fresh_near)):
        (x_block, x_at), (in_block, in_at) = places[at]
        value = finished(
            own[at],
            [block[at] for block in received],
            blocks[in_block][in_at],
            blocks[x_block][x_at],
            gain[...],
        )
        if at == 0:
            result[...] = value
        outgoing[at] = jnp.where(lax.axis_index("section") == 0, extra[tick], value)


def finish(own, received, blocks, places, gain, fresh, fresh_near, tick, after):
    pair, rows, width = own.shape
    operands = [gain, fresh, fresh_near, *blocks, own, *received]
    return pl.pallas_call(
        functools.partial(finish_kernel, places, (len(blocks), 1 + len(received)), tick),
        out_shape=(shape_of((rows, width), bf16), shape_of((pair, rows, width), bf16)),
        in_specs=[VMEM] * len(operands) + [ANY],
        out_specs=(VMEM, VMEM),
        compiler_params=limit(6),
        name="finish",
    )(*operands, after)


def end_kernel(places, count, gain, x_rows, incoming, own, *refs):
    received, (*past, out) = refs[:count], refs[count:]
    for before, value in enumerate(past):
        out[before, 0] = value[...]
    received = [block[...] for block in received]
    x_at, in_at = places
    out[len(past), 0] = finished(own[...], received, incoming[in_at], x_rows[x_at], gain[...])


def end(own, received, x_rows, incoming, places, gain, past):
    operands = [gain, x_rows, incoming, own, *received, *past]
    return pl.pallas_call(
        functools.partial(end_kernel, places, len(received)),
        out_shape=shape_of((len(past) + 1, 1, *own.shape), bf16),
        in_specs=[VMEM] * len(operands),
        out_specs=VMEM,
        compiler_params=limit(6),
        name="end",
    )(*operands)


def body(stash, w_in, w_out, gain, plan, arriving, fresh):
    ticks, rows = plan.shape[0], stash.shape[2]
    parts = lax.axis_size("tp")
    masks = range(2, parts, 2)
    weights = (w_in, w_out)
    order = [(which, piece) for which in (0, 1) for piece in range(PIECES)]
    stages = [order[:FIRST], order[FIRST:SECOND], order[SECOND:]]

    first, later = pick(plan, stash)
    moved = from_mirror(first)
    loaded, token = load(weights, stages[0], first)
    later, fresh_near = tie([later, fresh], token)
    later, fresh_near = from_mirror(later), swapped(fresh_near, masks[0])
    packed = pack(moved, arriving, token)
    chips = [swapped(packed, mask) for mask in masks]
    more, token = load(weights, stages[1], packed)
    loaded += more
    chips = tie(chips, token)
    gathered = with_cores([packed, *chips])
    x_blocks, x_places = gathered, [(block, 0) for block in range(parts)]
    in_blocks, in_places = gathered, [(block, 1) for block in range(parts)]

    (later,) = tie([later], token)
    near = swapped(later, masks[0])
    w_ins, w_outs = loaded[:PIECES], loaded[PIECES:]
    gates, more, token = gate(
        x_blocks, x_places, gain, w_ins, 1024, weights, stages[2], w_outs
    )
    w_outs += more
    later = double(later, near, token)
    for mask in masks[1:]:
        if mask & (mask - 1) == 0:
            near = swapped(later, mask)
            if 2 * mask < parts:
                later = double(later, near, token)

    results = []
    for tick in range(ticks):
        last = tick + 1 == ticks
        own, other = back(in_blocks, in_places, gates, w_outs, w_ins, 512)
        if tick == 0:
            later = double(later, near, own)
            later = [later, swapped(later, 1)]
        blocks = fold(own, swapped(other, 1), rows, not last)
        received = [swapped(block, mask) for block, mask in zip(blocks[1:], masks)]
        if last:
            places = (x_places[0][1], in_places[0][1])
            return end(blocks[0], received, x_blocks[0], in_blocks[0], places, gain, results)
        next_places = [(block, (chip, tick)) for block in (0, 1) for chip in range(parts // 2)]
        half = PIECES // 2
        gates_a, _, token = gate(
            later, next_places, gain, w_ins[:half], 1024, weights, [], (blocks[0], *w_outs)
        )
        places, used = [], []
        for at in (0, 1):
            places.append([])
            for from_blocks, from_places in ((x_blocks, x_places), (in_blocks, in_places)):
                block, where = from_places[at]
                places[at].append((len(used), where))
                used.append(from_blocks[block])
        result, outgoing = finish(
            blocks[0], received, used, places, gain, fresh, fresh_near, tick, token
        )
        results.append(result)
        came = [from_above(outgoing, mask) for mask in range(0, parts, 4)]
        gates_b, _, token = gate(
            later, next_places, gain, w_ins[half:], 1024, weights, [], (outgoing, *w_outs)
        )
        gates = gates_a + gates_b
        in_blocks = with_cores(list(tie(came, token)))
        in_places = [(block, at) for block in range(parts // 2) for at in (0, 1)]
        x_blocks, x_places = later, next_places


def solution(mesh):
    placed = (
        P("section", None, "tp", None),
        P("section", None, "tp"),
        P("section", "tp", None),
        P("section", None),
        P(),
        P("section", "tp", None),
        P(None, "tp", None),
    )
    return jax.shard_map(
        body, mesh=mesh, in_specs=placed, out_specs=P(None, "section", "tp", None), check_vma=False
    )
```

```python
import functools

import jax
import jax.numpy as jnp
from jax import lax
from jax.experimental import pallas as pl
from jax.experimental.pallas import tpu as pltpu
from jax.sharding import PartitionSpec as P

epsilon = 1e-06
MIB = 2**20
f32 = jnp.float32
bf16 = jnp.bfloat16
VMEM = pl.BlockSpec(memory_space=pltpu.VMEM)
HBM = pl.BlockSpec(memory_space=pltpu.HBM)
SMEM = pl.BlockSpec(memory_space=pltpu.SMEM)
ANY = pl.BlockSpec(memory_space=pl.ANY)


def shape_of(shape, dtype):
    return jax.ShapeDtypeStruct(shape, dtype)


def limit(mib):
    return pltpu.CompilerParams(vmem_limit_bytes=mib * MIB)


def in_vmem(value):
    return pltpu.with_memory_space_constraint(value, pltpu.VMEM)


def in_hbm(value):
    return pltpu.with_memory_space_constraint(value, pltpu.HBM)


def swapped(value, mask):
    return lax.ppermute(value, "tp", [(i, i ^ mask) for i in range(lax.axis_size("tp"))])


def from_mirror(value):
    count = lax.axis_size("section")
    return lax.ppermute(value, "section", [(i, (i + count // 2) % count) for i in range(count)])


def from_above(value, mask):
    sections, parts = lax.axis_size("section"), lax.axis_size("tp")
    pairs = [
        (((s + 1) % sections) * parts + (i ^ mask), s * parts + i)
        for s in range(sections)
        for i in range(parts)
    ]
    return lax.ppermute(value, ("section", "tp"), pairs)


def with_cores(chips):
    return chips + [swapped(value, 1) for value in chips]


def pick_kernel(plan, stash, first, later, slots, stored, sems):
    sections = lax.axis_size("section")
    partner = lax.rem(lax.axis_index("section") + sections // 2, sections)
    copies = [
        pltpu.make_async_copy(plan, slots, sems.at[0]),
        pltpu.make_async_copy(stash.at[0], stored, sems.at[1]),
    ]
    for copy in copies:
        copy.start()
    for copy in copies:
        copy.wait()
    first[...] = stored[slots[0, partner]]
    for tick in range(later.shape[1]):
        later[0, tick] = stored[slots[tick + 1, partner]]


def pick(plan, stash):
    ticks, (_, _, rows, width) = plan.shape[0], stash.shape
    return pl.pallas_call(
        pick_kernel,
        out_shape=(
            shape_of((rows, width), stash.dtype),
            shape_of((1, ticks - 1, rows, width), stash.dtype),
        ),
        in_specs=[HBM, HBM],
        out_specs=(VMEM, VMEM),
        scratch_shapes=[
            pltpu.SMEM(plan.shape, plan.dtype),
            pltpu.VMEM(stash.shape[1:], stash.dtype),
            pltpu.SemaphoreType.DMA((2,)),
        ],
        compiler_params=limit(6),
        name="pick",
    )(in_hbm(plan), in_hbm(stash))


PIECES = 8
FIRST, SECOND = 5, 11


def piece_copies(wanted, weights, outs, sems):
    copies = []
    for at, ((which, piece), out) in enumerate(zip(wanted, outs)):
        where = [slice(None), slice(None)]
        axis = 1 - which
        where[axis] = pl.ds(piece * out.shape[axis], out.shape[axis])
        copies.append(pltpu.make_async_copy(weights[which].at[0, *where], out, sems.at[at]))
    return copies


def piece_shapes(wanted, weights):
    shapes = []
    for which, _ in wanted:
        shape = list(weights[which].shape[1:])
        shape[1 - which] //= PIECES
        shapes.append(pltpu.VMEM(tuple(shape), weights[which].dtype))
    return shapes


def load_kernel(wanted, w_in, w_out, after, *refs):
    *outs, token, sems = refs
    copies = piece_copies(wanted, (w_in, w_out), outs, sems)
    for copy in copies:
        copy.start()
    token[...] = jnp.zeros_like(token)
    for copy in copies:
        copy.wait()


def load(weights, wanted, after):
    shapes = piece_shapes(wanted, weights)
    *pieces, token = pl.pallas_call(
        functools.partial(load_kernel, wanted),
        out_shape=(*shapes, shape_of((8, 128), f32)),
        in_specs=[HBM, HBM, ANY],
        out_specs=tuple([VMEM] * (len(wanted) + 1)),
        scratch_shapes=[pltpu.SemaphoreType.DMA((len(wanted),))],
        compiler_params=limit(6),
        cost_estimate=pl.CostEstimate(
            flops=0,
            bytes_accessed=4 * sum(shape.shape[0] * shape.shape[1] for shape in shapes),
            transcendentals=0,
        ),
        name="load",
    )(*[in_hbm(weight) for weight in weights], after)
    return pieces, token


def tie_kernel(*refs):
    pass


def tie(values, token):
    return pl.pallas_call(
        tie_kernel,
        out_shape=tuple(shape_of(value.shape, value.dtype) for value in values),
        in_specs=[ANY] * (len(values) + 1),
        out_specs=tuple([ANY] * len(values)),
        input_output_aliases={at: at for at in range(len(values))},
        compiler_params=limit(1),
        name="tie",
    )(*values, token)


def pack_kernel(one, other, after, out):
    out[0] = one[...]
    out[1] = other[0]


def pack(one, other, after):
    return pl.pallas_call(
        pack_kernel,
        out_shape=shape_of((2, *one.shape), one.dtype),
        in_specs=[VMEM, VMEM, ANY],
        out_specs=VMEM,
        compiler_params=limit(6),
        name="pack",
    )(one, other, after)


def double_kernel(one, other, after, out):
    count = one.shape[0]
    out[:count] = one[...]
    out[count:] = other[...]


def double(one, other, after):
    count, *block = one.shape
    return pl.pallas_call(
        double_kernel,
        out_shape=shape_of((2 * count, *block), one.dtype),
        in_specs=[VMEM, VMEM, ANY],
        out_specs=VMEM,
        compiler_params=limit(6),
        name="double",
    )(one, other, after)


def joined(blocks, places):
    return jnp.concatenate([blocks[block][at].astype(f32) for block, at in places], axis=0)


def for_kernel(blocks, places):
    if blocks[0].shape[-2] % 8 == 0:
        return list(blocks), places
    return [joined(blocks, places).astype(bf16)], [(0, ...)]


def normalised(values):
    inverse_rms = lax.rsqrt(jnp.mean(values * values, axis=-1, keepdims=True) + epsilon)
    return inverse_rms, values * inverse_rms


def gate_values(inputs, w_in, part):
    preact = jnp.dot(inputs, w_in[:, part], preferred_element_type=f32)
    return (2.0 * jnp.maximum(preact, 0.0)).T


def spans(size, chunk):
    chunk = min(chunk, size)
    return [pl.ds(at, chunk) for at in range(0, size, chunk)]


def gate_kernel(places, counts, wanted, chunk, *refs):
    blocks, refs = refs[: counts[0]], refs[counts[0] :]
    gain, w_ins, refs = refs[0], refs[1 : 1 + counts[1]], refs[1 + counts[1] :]
    weights, refs = refs[:2], refs[2 + counts[2] :]
    gates, outs, (token, sems) = refs[: counts[1]], refs[counts[1] : -2], refs[-2:]
    copies = piece_copies(wanted, weights, outs, sems)
    for copy in copies:
        copy.start()
    token[...] = jnp.zeros_like(token)
    inputs = (normalised(joined(blocks, places))[1] * gain[...]).astype(bf16)
    for w_in, out in zip(w_ins, gates):
        for part in spans(out.shape[0], chunk):
            out[part, :] = gate_values(inputs, w_in, part).astype(bf16)
    for copy in copies:
        copy.wait()


def gate(blocks, places, gain, w_ins, chunk, weights, wanted, after):
    blocks, places = for_kernel(blocks, places)
    tokens = sum(block.shape[-2] for block in blocks) if places == [(0, ...)] else None
    if tokens is None:
        tokens = len(places) * blocks[0].shape[-2]
    width, hidden = w_ins[0].shape
    count = len(w_ins)
    *outs, token = pl.pallas_call(
        functools.partial(gate_kernel, places, (len(blocks), count, len(after)), wanted, chunk),
        out_shape=(
            *[pltpu.VMEM((hidden, tokens), bf16)] * count,
            *piece_shapes(wanted, weights),
            shape_of((8, 128), f32),
        ),
        in_specs=[VMEM] * (len(blocks) + 1 + count) + [HBM] * 2 + [ANY] * len(after),
        out_specs=tuple([VMEM] * (count + len(wanted) + 1)),
        scratch_shapes=[pltpu.SemaphoreType.DMA((max(len(wanted), 1),))],
        compiler_params=limit(6),
        cost_estimate=pl.CostEstimate(
            flops=2 * tokens * width * hidden * count,
            bytes_accessed=(2 * width + 2 * tokens) * hidden * count,
            transcendentals=0,
        ),
        name="gate",
    )(
        *blocks,
        gain,
        *[in_vmem(piece) for piece in w_ins],
        *[in_hbm(weight) for weight in weights],
        *after,
    )
    return outs[:count], outs[count:], token


def back_kernel(places, count, chunk, *refs):
    blocks, (*operands, own, other) = refs[:count], refs[count:]
    w_outs, w_ins, gates = [operands[at : at + PIECES] for at in range(0, 3 * PIECES, PIECES)]
    incoming = joined(blocks, places).T.astype(bf16)
    total = None
    for w_out, w_in, gate_piece in zip(w_outs, w_ins, gates):
        for part in spans(w_out.shape[0], chunk):
            hidden_back = jnp.dot(w_out[part, :], incoming, preferred_element_type=f32)
            hidden_grad = (hidden_back * gate_piece[part, :].astype(f32)).astype(bf16)
            partial = jnp.dot(w_in[:, part], hidden_grad, preferred_element_type=f32)
            total = partial if total is None else total + partial
    sums = total.T
    rows = own.shape[0]
    own[...] = sums[:rows]
    other[...] = sums[rows:].astype(bf16)


def back(blocks, places, gates, w_outs, w_ins, chunk):
    blocks, places = for_kernel(blocks, places)
    tokens = gates[0].shape[1]
    width, hidden = w_ins[0].shape
    hidden *= PIECES
    operands = [*blocks, *[in_vmem(piece) for piece in (*w_outs, *w_ins, *gates)]]
    return pl.pallas_call(
        functools.partial(back_kernel, places, len(blocks), chunk),
        out_shape=(
            shape_of((tokens // 2, width), f32),
            shape_of((tokens // 2, width), bf16),
        ),
        in_specs=[VMEM] * len(operands),
        out_specs=(VMEM, VMEM),
        compiler_params=limit(6),
        cost_estimate=pl.CostEstimate(
            flops=4 * tokens * width * hidden,
            bytes_accessed=4 * width * hidden + 2 * tokens * hidden,
            transcendentals=0,
        ),
        name="back",
    )(*operands)


def fold_values(own, received, rows, near):
    sums = own + received.astype(f32)
    blocks = [sums[at : at + rows] for at in range(0, sums.shape[0], rows)]
    if not near:
        return blocks[:1] + [block.astype(bf16) for block in blocks[1:]]
    pairs = [jnp.stack([blocks[at], blocks[at ^ 1]]) for at in range(len(blocks))]
    return pairs[:1] + [pair.astype(bf16) for pair in pairs[1:]]


def fold_kernel(rows, near, own, received, *outs):
    for out, value in zip(outs, fold_values(own[...], received[...], rows, near)):
        out[...] = value


def fold(own, received, rows, near):
    if rows % 8:
        return fold_values(own, received, rows, near)
    half, width = own.shape
    shape = (2, rows, width) if near else (rows, width)
    return pl.pallas_call(
        functools.partial(fold_kernel, rows, near),
        out_shape=tuple(shape_of(shape, bf16 if at else f32) for at in range(half // rows)),
        in_specs=[VMEM] * 2,
        out_specs=tuple([VMEM] * (half // rows)),
        compiler_params=limit(6),
        name="fold",
    )(own, received)


def finished(own, received, incoming, x_rows, gain):
    total = own
    for block in received:
        total = total + block.astype(f32)
    inverse_rms, normed = normalised(x_rows.astype(f32))
    scaled = total * gain
    inner = jnp.mean(scaled * normed, axis=-1, keepdims=True)
    return (incoming.astype(f32) + inverse_rms * (scaled - normed * inner)).astype(bf16)


def finish_kernel(places, count, tick, gain, fresh, fresh_near, *refs):
    blocks, refs = refs[: count[0]], refs[count[0] :]
    own, received, (_, result, outgoing) = refs[0], refs[1 : count[1]], refs[count[1] :]
    for at, extra in enumerate((fresh, fresh_near)):
        (x_block, x_at), (in_block, in_at) = places[at]
        value = finished(
            own[at],
            [block[at] for block in received],
            blocks[in_block][in_at],
            blocks[x_block][x_at],
            gain[...],
        )
        if at == 0:
            result[...] = value
        outgoing[at] = jnp.where(lax.axis_index("section") == 0, extra[tick], value)


def finish(own, received, blocks, places, gain, fresh, fresh_near, tick, after):
    pair, rows, width = own.shape
    operands = [gain, fresh, fresh_near, *blocks, own, *received]
    return pl.pallas_call(
        functools.partial(finish_kernel, places, (len(blocks), 1 + len(received)), tick),
        out_shape=(shape_of((rows, width), bf16), shape_of((pair, rows, width), bf16)),
        in_specs=[VMEM] * len(operands) + [ANY],
        out_specs=(VMEM, VMEM),
        compiler_params=limit(6),
        name="finish",
    )(*operands, after)


def end_kernel(places, count, gain, x_rows, incoming, own, *refs):
    received, (*past, out) = refs[:count], refs[count:]
    for before, value in enumerate(past):
        out[before, 0] = value[...]
    received = [block[...] for block in received]
    x_at, in_at = places
    out[len(past), 0] = finished(own[...], received, incoming[in_at], x_rows[x_at], gain[...])


def end(own, received, x_rows, incoming, places, gain, past):
    operands = [gain, x_rows, incoming, own, *received, *past]
    return pl.pallas_call(
        functools.partial(end_kernel, places, len(received)),
        out_shape=shape_of((len(past) + 1, 1, *own.shape), bf16),
        in_specs=[VMEM] * len(operands),
        out_specs=VMEM,
        compiler_params=limit(6),
        name="end",
    )(*operands)


def body(stash, w_in, w_out, gain, plan, arriving, fresh):
    ticks, rows = plan.shape[0], stash.shape[2]
    parts = lax.axis_size("tp")
    masks = range(2, parts, 2)
    weights = (w_in, w_out)
    order = [(which, piece) for which in (0, 1) for piece in range(PIECES)]
    stages = [order[:FIRST], order[FIRST:SECOND], order[SECOND:]]

    first, later = pick(plan, stash)
    moved = from_mirror(first)
    loaded, token = load(weights, stages[0], first)
    later, fresh_near = tie([later, fresh], token)
    later, fresh_near = from_mirror(later), swapped(fresh_near, masks[0])
    packed = pack(moved, arriving, token)
    chips = [swapped(packed, mask) for mask in masks]
    more, token = load(weights, stages[1], packed)
    loaded += more
    chips = [tie([value], token)[0] for value in chips]
    gathered = with_cores([packed, *chips])
    x_blocks, x_places = gathered, [(block, 0) for block in range(parts)]
    in_blocks, in_places = gathered, [(block, 1) for block in range(parts)]

    (later,) = tie([later], token)
    near = swapped(later, masks[0])
    w_ins, w_outs = loaded[:PIECES], loaded[PIECES:]
    gates, more, token = gate(
        x_blocks, x_places, gain, w_ins, 1024, weights, stages[2], w_outs
    )
    w_outs += more
    later = double(later, near, token)
    for mask in masks[1:]:
        if mask & (mask - 1) == 0:
            near = swapped(later, mask)
            if 2 * mask < parts:
                later = double(later, near, token)

    results = []
    for tick in range(ticks):
        last = tick + 1 == ticks
        own, other = back(in_blocks, in_places, gates, w_outs, w_ins, 512)
        if tick == 0:
            later = double(later, near, own)
            later = [later, swapped(later, 1)]
        blocks = fold(own, swapped(other, 1), rows, not last)
        received = [swapped(block, mask) for block, mask in zip(blocks[1:], masks)]
        if last:
            places = (x_places[0][1], in_places[0][1])
            return end(blocks[0], received, x_blocks[0], in_blocks[0], places, gain, results)
        next_places = [(block, (chip, tick)) for block in (0, 1) for chip in range(parts // 2)]
        half = PIECES // 2
        gates_a, _, token = gate(
            later, next_places, gain, w_ins[:half], 1024, weights, [], (blocks[0], *w_outs)
        )
        places, used = [], []
        for at in (0, 1):
            places.append([])
            for from_blocks, from_places in ((x_blocks, x_places), (in_blocks, in_places)):
                block, where = from_places[at]
                places[at].append((len(used), where))
                used.append(from_blocks[block])
        result, outgoing = finish(
            blocks[0], received, used, places, gain, fresh, fresh_near, tick, token
        )
        results.append(result)
        came = [from_above(outgoing, mask) for mask in range(0, parts, 4)]
        gates_b, _, token = gate(
            later, next_places, gain, w_ins[half:], 1024, weights, [], (outgoing, *w_outs)
        )
        gates = gates_a + gates_b
        in_blocks = with_cores([tie([value], token)[0] for value in came])
        in_places = [(block, at) for block in range(parts // 2) for at in (0, 1)]
        x_blocks, x_places = later, next_places


def solution(mesh):
    placed = (
        P("section", None, "tp", None),
        P("section", None, "tp"),
        P("section", "tp", None),
        P("section", None),
        P(),
        P("section", "tp", None),
        P(None, "tp", None),
    )
    return jax.shard_map(
        body, mesh=mesh, in_specs=placed, out_specs=P(None, "section", "tp", None), check_vma=False
    )
```
